128 devices in a mesh: dp: 16 (over z, y), expert: 8 (over x, core).
Axes of the slice: x: 4, y: 4, z: 4, core: 2. Of those that a mesh axis runs over, the one named last changes fastest.
Arguments:
- inputs: bfloat16 [8192, 2048], P('dp', 'expert'), may hold values from -6 to 6
- grad_output: bfloat16 [8192, 2048], P('dp', 'expert'), may hold values from -6 to 6
- gates: bfloat16 [8192, 8], P('dp'), may hold values from 0.019897461 to 0.3984375
- expert_ids: int32 [8192, 8], P('dp'), may hold values from 0 to 127, all different within a row; in each aligned block of 512 rows (0 to 511, 512 to 1023, ...) at most 64 rows name the same one
- owner: int32 [128], replicated, may hold values from 0 to 127, each once
- w_gate: bfloat16 [128, 2048, 768], P(('dp', 'expert')), may hold values from -0.125 to 0.125
- w_up: bfloat16 [128, 2048, 768], P(('dp', 'expert')), may hold values from -0.125 to 0.125
- w_down: bfloat16 [128, 768, 2048], P(('dp', 'expert')), may hold values from -0.21875 to 0.21875
Outputs:
- grad_inputs: bfloat16 [8192, 2048], P('dp', 'expert')
- grad_gates: bfloat16 [8192, 8], P('dp')
- grad_w_gate: bfloat16 [128, 2048, 768], P(('dp', 'expert'))
- grad_w_up: bfloat16 [128, 2048, 768], P(('dp', 'expert'))
- grad_w_down: bfloat16 [128, 768, 2048], P(('dp', 'expert'))
The draws below stay inside these ranges and needn't reach their ends.
Inputs may be any that keep to these rules, and one draw needn't show every extreme that they name: `expert_ids`: in each aligned block of 512 tokens no expert is named by more than 64 slots, and in some block one expert is named by exactly 64; a token names 8 different experts. `owner`: each storage slot holds exactly one expert; slot s lies on the device of index s along dp+expert.
All inputs are finite; a program needn't handle non-finite values.
Results may differ from the reference program's by a relative error of at most 0.012.
Values may be sent and summed in bfloat16 or wider, within the bound.
A program may use at most 128 MiB of HBM per device.

```python
import math
import jax
import jax.numpy as jnp
import numpy as np
from jax import lax

D = 2048
FF = 768
TOP = 8
TOK_DEV = 512
EXPERTS = 128
CAP = 64
TOKENS = 8192
N_DP = 16


def block_levels(key, dims, shards, least, largest):
    factor_of, own = 1.0, jax.random.fold_in(key, 6)
    for axis_at, shards_of in shards:
        steps = jnp.exp(jax.random.uniform(jax.random.fold_in(own, axis_at), (shards_of,), jnp.float32, least / len(shards), largest / len(shards)))
        factor_of = factor_of * jnp.repeat(steps, dims[axis_at] // shards_of).reshape([-1 if axis == axis_at else 1 for axis in range(len(dims))])
    return factor_of


def deal_out(own_key, own, number, rows, amount, top, most, skew):
    ranking = jax.random.permutation(own_key, amount)
    packed, usual = portions_of(amount, rows * top, most, skew, True), portions_of(amount, rows * top, most, skew, False)
    places = jnp.arange(amount)

    def named(tallies, turn):
        used = int((tallies > 0).sum())
        fixed = max(1, used // 4)
        shifted = fixed + (places - fixed + turn * (used - fixed)) % max(1, amount - fixed)
        return jnp.zeros((amount,), jnp.int32).at[ranking[jnp.where(places < fixed, places, shifted)]].set(jnp.asarray(tallies, jnp.int32))

    tallies = jnp.where(number % 4 == 0, named(packed, number // 4), named(usual, number - number // 4 - 1))
    mixed = jax.random.permutation(jax.random.fold_in(own, 3), amount)
    source_of, sink = mixed[0:amount // 2 * 2:2], mixed[1:amount // 2 * 2:2]
    room = jnp.minimum(tallies[source_of] - 1, most - tallies[sink]) // 2
    room = jnp.where((source_of == ranking[0]) | (sink == ranking[0]) | (tallies[sink] == 0), 0, jnp.maximum(room, 0))
    shifted = jax.random.randint(jax.random.fold_in(own, 4), (amount // 2,), 0, 1 << 20) % (room + 1)
    tallies = tallies.at[source_of].add(-shifted).at[sink].add(shifted)
    members = jnp.searchsorted(jnp.cumsum(tallies), jnp.arange(rows * top), side="right").astype(jnp.int32)
    grid = members.reshape(top, rows).T
    grid = grid[jax.random.permutation(jax.random.fold_in(own, 1), rows)]
    turn = jax.random.randint(jax.random.fold_in(own, 2), (rows, 1), 0, top)
    return jnp.take_along_axis(grid, (jnp.arange(top)[None, :] + turn) % top, axis=1)


def portions_of(count, total, reach, skew, full):
    weights = [(1 << 20) // math.isqrt(rank ** skew) + 1 for rank in range(1, count + 1)]
    largest = reach if full else min(reach, max(-(-total // count), total * weights[0] // sum(weights)))
    least = 1 if total - largest >= count - 1 else 0
    given, rest = [largest] + [least] * (count - 1), total - largest - least * (count - 1)
    while rest > 0:
        candidates = [i for i in range(1, count) if given[i] < largest] or [i for i in range(1, count) if given[i] < reach]
        pool, left = sum([weights[i] for i in candidates]), rest
        for i in candidates:
            more = min(reach - given[i], max(1, left * weights[i] // pool), rest)
            given[i] = given[i] + more
            rest = rest - more
    return np.array(given)


def centred(key, shape, width, limit, pieces=(), kind=jnp.bfloat16):
    factor_of = block_levels(key, shape, pieces, -0.22, 0.18) if pieces else 1.0
    array = jax.random.normal(key, shape, jnp.float32) * width * factor_of
    return jnp.minimum(jnp.maximum(array, -limit), limit).astype(kind)


def setup_inputs(seed: int = 0) -> dict:
    streams_of = jax.random.split(jax.random.key(seed), 9)
    inputs = centred(streams_of[0], (TOKENS, D), 1.0, 6.0, ((0, 16), (1, 8)))
    grad_output = centred(streams_of[1], (TOKENS, D), 1.0, 6.0, ((0, 16), (1, 8)))
    gates = jnp.clip(0.019897461 + 0.37854004 * jax.random.uniform(streams_of[2], (TOKENS, TOP), jnp.float32) ** block_levels(streams_of[2], (TOKENS, TOP), ((0, 16),), -0.2, 0.2), 0.019897461, 0.3984375).astype(jnp.bfloat16)
    expert_ids_keys = jax.random.split(jax.random.fold_in(streams_of[3], 1), TOKENS // TOK_DEV)
    expert_ids_turns = jax.random.permutation(jax.random.fold_in(streams_of[3], 3), TOKENS // TOK_DEV)
    expert_ids = jax.vmap(lambda own, number: deal_out(jax.random.fold_in(streams_of[3], 2), own, number, TOK_DEV, EXPERTS, TOP, CAP, 2))(expert_ids_keys, expert_ids_turns).reshape((TOKENS, TOP))
    owner = jax.random.permutation(streams_of[4], EXPERTS).astype(jnp.int32)
    w_gate = centred(streams_of[5], (EXPERTS, D, FF), D ** -0.5, 0.125, ((0, 128),))
    w_up = centred(streams_of[6], (EXPERTS, D, FF), D ** -0.5, 0.125, ((0, 128),))
    w_down = centred(streams_of[7], (EXPERTS, FF, D), FF ** -0.5, 0.21875, ((0, 128),))
    return {"inputs": inputs, "grad_output": grad_output, "gates": gates, "expert_ids": expert_ids, "owner": owner, "w_gate": w_gate, "w_up": w_up, "w_down": w_down}


def contract(left, right, dim_left, dim_right):
    return lax.dot_general(left, right, (((dim_left,), (dim_right,)), ((), ())), preferred_element_type=jnp.float32)


def expert_backward(rows, grads, weights_g, weight_gate, weight_up, weight_down):
    h1 = contract(rows, weight_gate, 1, 0)
    h2 = contract(rows, weight_up, 1, 0)
    sigma = jax.nn.sigmoid(h1)
    act = h1 * sigma
    slope = sigma * (1.0 + h1 * (1.0 - sigma))
    acted = (act * h2).astype(jnp.bfloat16)
    dz = contract(grads, weight_down, 1, 1)
    grad_gate_rows = jnp.sum(acted.astype(jnp.float32) * dz, axis=1).astype(jnp.bfloat16)
    gate_col = weights_g.astype(jnp.float32)[:, None]
    scaled = (gate_col * grads.astype(jnp.float32)).astype(jnp.bfloat16)
    grad_down = contract(acted, scaled, 0, 0).astype(jnp.bfloat16)
    dfa = gate_col * dz
    dh_gate = (dfa * h2 * slope).astype(jnp.bfloat16)
    dh_up = (dfa * act).astype(jnp.bfloat16)
    grad_gate = contract(rows, dh_gate, 0, 0).astype(jnp.bfloat16)
    grad_up = contract(rows, dh_up, 0, 0).astype(jnp.bfloat16)
    slot_grad = (contract(dh_gate, weight_gate, 1, 1) + contract(dh_up, weight_up, 1, 1)).astype(jnp.bfloat16)
    return grad_gate, grad_up, grad_down, slot_grad, grad_gate_rows


def reference(inputs, grad_output, gates, expert_ids, owner, w_gate, w_up, w_down):
    slots = owner[expert_ids].reshape(-1).astype(jnp.int32)
    total = slots.shape[0]
    cap_all = N_DP * CAP
    onehot = (slots[:, None] == jnp.arange(EXPERTS, dtype=jnp.int32)[None, :]).astype(jnp.int32)
    ranks = jnp.sum(jnp.cumsum(onehot, axis=0) * onehot, axis=1) - 1
    places = (slots * cap_all + ranks).astype(jnp.int32)
    table = jnp.full((EXPERTS * cap_all,), total, jnp.int32).at[places].set(jnp.arange(total, dtype=jnp.int32))
    table = table.reshape(EXPERTS, cap_all)
    valid = table < total
    safe = jnp.where(valid, table, 0).astype(jnp.int32)
    token_of = (safe // TOP).astype(jnp.int32)
    gate_rows = jnp.where(valid, gates.reshape(-1)[safe], jnp.zeros((), gates.dtype))

    def per_expert(items):
        tokens_here, gate_here, weight_gate, weight_up, weight_down = items
        return expert_backward(inputs[tokens_here], grad_output[tokens_here], gate_here, weight_gate, weight_up, weight_down)

    grad_gate, grad_up, grad_down, slot_grad, gate_grad_rows = lax.map(per_expert, (token_of, gate_rows, w_gate, w_up, w_down))
    live = valid[:, :, None]
    summed = jnp.zeros((TOKENS, D), jnp.float32).at[token_of.reshape(-1)].add(
        jnp.where(live, slot_grad.astype(jnp.float32), 0.0).reshape(-1, D))
    target = jnp.where(valid, table, total).reshape(-1).astype(jnp.int32)
    flat = jnp.zeros((total,), jnp.float32).at[target].set(gate_grad_rows.astype(jnp.float32).reshape(-1), mode="drop")
    grad_gates = flat.reshape(TOKENS, TOP).astype(jnp.bfloat16)
    return summed.astype(jnp.bfloat16), grad_gates, grad_gate, grad_up, grad_down
```

```python
import jax
import jax.numpy as jnp
from jax import lax
from jax.experimental import pallas as pl
from jax.experimental.pallas import tpu as pltpu
from jax.sharding import PartitionSpec as P

D, FF, TOP, TOK, CAP = 2048, 768, 8, 512, 64
HALF = CAP // 2
SH = 256
WIDE = D + 128
SLOTS = 1024
SEMS = 160
BF, F32 = jnp.bfloat16, jnp.float32
MESH = pl.DeviceIdType.MESH
ORDER = (1, 3, 2)


def dot(left, right, dim_left, dim_right):
    return lax.dot_general(
        left, right, (((dim_left,), (dim_right,)), ((), ())), preferred_element_type=F32
    )


def iota(shape, dim):
    return lax.broadcasted_iota(jnp.int32, shape, dim).astype(F32)


def kernel(
    inp, gro, ids, gates, owner, wg_in, wu_in, wd_in,
    out_in, out_gates, out_wg, out_wu, out_wd,
    xin, ag, slots, gpack, grecv, pack, st1, st2, fin, wg, wu, wd, dz, act, dhg, dhu,
    bst1, bst2, back, pmat, tri, rall, onehot, core_in, rs_in, gsend, grecv_gates,
    send_sem, recv_sem, local_sem,
):
    row, col = lax.axis_index("dp"), lax.axis_index("expert")
    z, y = row // 4, row % 4
    x, c = col // 2, col % 2
    counts = {"remote": 0, "local": 0}

    def at(k, base):
        return (base + k + 4) % 4

    def zdev(k):
        return (at(k, z) * 4 + y, col)

    def ydev(k):
        return (z * 4 + at(k, y), col)

    def xdev(k, flip):
        return (row, at(k, x) * 2 + (c + flip) % 2)

    def send(src, dst, device):
        n = counts["remote"]
        counts["remote"] = n + 1
        copy = pltpu.make_async_remote_copy(
            src_ref=src, dst_ref=dst, send_sem=send_sem.at[n], recv_sem=recv_sem.at[n],
            device_id=device, device_id_type=MESH,
        )
        copy.start()
        return copy

    def local(src, dst):
        n = counts["local"]
        counts["local"] = n + 1
        copy = pltpu.make_async_copy(src, dst, local_sem.at[n])
        copy.start()
        return copy

    weights = [local(wg_in, wg), local(wu_in, wu), local(wd_in, wd)]
    own_in, own_gro = local(inp, xin.at[col]), local(gro, ag.at[row])

    barrier = pltpu.get_barrier_semaphore()
    peers = [zdev(k) for k in ORDER] + [ydev(k) for k in ORDER]
    peers += [xdev(k, f) for k in range(4) for f in range(2) if (k, f) != (0, 0)]
    for peer in peers:
        pl.semaphore_signal(barrier, inc=1, device_id=peer, device_id_type=MESH)
    pl.semaphore_wait(barrier, len(peers))

    x_own = [send(inp, xin.at[col], xdev(k, 0)) for k in ORDER]
    x_core = [send(inp, xin.at[col], xdev(0, 1))]
    lower, upper = pl.ds(0, TOK // 2), pl.ds(TOK // 2, TOK // 2)
    a_one = [send(gro.at[lower], ag.at[row, lower], ydev(k)) for k in ORDER]
    b_one = [send(gro.at[upper], ag.at[row, upper], zdev(k)) for k in ORDER]
    a_two = {0: [send(gro.at[lower], ag.at[row, lower], zdev(k)) for k in ORDER]}
    b_two = {0: [send(gro.at[upper], ag.at[row, upper], ydev(k)) for k in ORDER]}

    tri[...] = (iota((TOK, TOK), 0) <= iota((TOK, TOK), 1)).astype(BF)
    expert_no = lax.broadcasted_iota(jnp.int32, (128, TOK), 0)
    owner_row = jnp.broadcast_to(owner[...].astype(F32), (8, 128)).astype(BF)
    for k in range(TOP):
        match = (ids[k : k + 1, :] == expert_no).astype(F32).astype(BF)
        slots[row, k : k + 1, :] = dot(owner_row, match, 1, 0)[0:1, :]
    s_one = [send(slots.at[row], slots.at[row], ydev(k)) for k in ORDER]

    mine = slots[row]
    name = iota((16, TOK), 0) * 8.0 + col.astype(F32)
    member = jnp.zeros((16, TOK), F32)
    gate_of = jnp.zeros((16, TOK), F32)
    for k in range(TOP):
        hit = mine[k : k + 1, :] == name
        member += jnp.where(hit, 1.0, 0.0)
        gate_of += jnp.where(hit, gates[k : k + 1, :].astype(F32), 0.0)
    rank = dot(member.astype(BF), tri[...], 1, 0) * member
    place = iota((CAP, TOK), 0) + 1.0
    for d in range(16):
        hot = jnp.where(rank[d : d + 1, :] == place, 1.0, 0.0)
        pmat[d * CAP : (d + 1) * CAP, :] = hot.astype(BF)
        gate_col = jnp.sum(hot * gate_of[d : d + 1, :], axis=1, keepdims=True)
        pack[d // 4, d % 4, :, D:WIDE] = jnp.broadcast_to(gate_col, (CAP, 128)).astype(BF)

    for copy in s_one:
        copy.wait_recv()
    s_two = [
        send(slots.at[pl.ds(z * 4, 4)], slots.at[pl.ds(z * 4, 4)], zdev(k)) for k in ORDER
    ]
    for n, k in enumerate(ORDER):
        x_own[n].wait_recv()
        source = at(-k, x) * 2 + c
        x_core.append(send(xin.at[source], xin.at[source], xdev(0, 1)))
        a_one[n].wait_recv()
        source = z * 4 + at(-k, y)
        a_two[k] = [
            send(ag.at[source, lower], ag.at[source, lower], zdev(m)) for m in ORDER
        ]
        b_one[n].wait_recv()
        source = at(-k, z) * 4 + y
        b_two[k] = [
            send(ag.at[source, upper], ag.at[source, upper], ydev(m)) for m in ORDER
        ]

    for copy in x_core:
        copy.wait_recv()
    own_in.wait()

    def pack_inputs(shard, _):
        rows = dot(pmat[...], xin[shard], 1, 0).astype(BF)
        pack[:, :, :, pl.ds(pl.multiple_of(shard * SH, SH), SH)] = rows.reshape(4, 4, CAP, SH)
        return 0

    lax.fori_loop(0, 8, pack_inputs, 0)

    first, second = pl.ds(0, HALF), pl.ds(HALF, HALF)
    p_one = [send(pack.at[:, at(k, y), first], st1.at[y], ydev(k)) for k in ORDER]
    q_one = [send(pack.at[at(k, z), :, second], st2.at[z], zdev(k)) for k in ORDER]
    p_two = {0: [send(pack.at[at(k, z), y, first], fin.at[z, y, first], zdev(k)) for k in ORDER]}
    q_two = {0: [send(pack.at[z, at(k, y), second], fin.at[z, y, second], ydev(k)) for k in ORDER]}
    own_rows = [local(pack.at[z, y], fin.at[z, y])]

    for copy in s_two:
        copy.wait_recv()
    own_gro.wait()
    near = iota((8, TOK), 0) + row.astype(F32) * 8.0

    def find_members(r, _):
        found = jnp.zeros((8, TOK), F32)
        theirs = slots[r]
        for k in range(TOP):
            found += jnp.where(theirs[k : k + 1, :] == near, 1.0, 0.0)
        rall[pl.ds(pl.multiple_of(r * 8, 8), 8), :] = found
        return 0

    lax.fori_loop(0, 16, find_members, 0)
    rall[...] = dot(rall[...].astype(BF), tri[...], 1, 0) * rall[...]

    def pack_gradients(group):
        def one(step, _):
            r = group * 4 + step
            ranks = rall[pl.ds(pl.multiple_of(r * 8, 8), 8), :]
            for e in range(8):
                hot = jnp.where(ranks[e : e + 1, :] == place, 1.0, 0.0)
                onehot[e * CAP : (e + 1) * CAP, :] = hot.astype(BF)
            rows = dot(onehot[...], ag[r], 1, 0).astype(BF)
            gpack[:, group, step] = rows.reshape(8, CAP, SH)
            return 0

        lax.fori_loop(0, 4, one, 0)

    g_sent = {}
    own_grads = []

    def exchange_gradients(group, k):
        for m in (0, 1, 3, 2):
            for f in range(2):
                target = at(m, x) * 2 + (c + f) % 2
                if (m, f) == (0, 0):
                    own_grads.append(local(gpack.at[col, group], grecv.at[col, group]))
                else:
                    g_sent[k, m, f] = send(
                        gpack.at[target, group], grecv.at[col, group], xdev(m, f)
                    )

    for k in (0, 1, 3, 2):
        if k == 0:
            for copy in b_two[0]:
                copy.wait_recv()
        else:
            b_seen = b_two[k]
            for copy in b_seen:
                copy.wait_recv()
            n = ORDER.index(k)
            for source in (0, 1, 3, 2):
                a_two[source][n].wait_recv()
        group = at(-k, z)
        pack_gradients(group)
        exchange_gradients(group, k)

    for n, k in enumerate(ORDER):
        p_one[n].wait_recv()
        source = at(-k, y)
        p_two[k] = [
            send(st1.at[source, at(m, z)], fin.at[z, source, first], zdev(m)) for m in ORDER
        ]
        own_rows.append(local(st1.at[source, z], fin.at[z, source, first]))
        q_one[n].wait_recv()
        source = at(-k, z)
        q_two[k] = [
            send(st2.at[source, at(m, y)], fin.at[source, y, second], ydev(m)) for m in ORDER
        ]
        own_rows.append(local(st2.at[source, y], fin.at[source, y, second]))

    for copy in weights:
        copy.wait()
    for copy in own_grads:
        copy.wait()

    def add_dz(shard, start):
        columns = pl.ds(pl.multiple_of(shard * SH, SH), SH)

        def chunk(n, _):
            rows = pl.ds(pl.multiple_of(n * 256, 256), 256)
            part = dot(grecv[shard, n].reshape(256, SH), wd[:, columns], 1, 1)
            dz[rows, :] = part if start else dz[rows, :] + part
            return 0

        lax.fori_loop(0, 4, chunk, 0)

    add_dz(col, True)
    for m in (0, 1, 3, 2):
        for f in range(2):
            if (m, f) != (0, 0):
                for k in (0, 1, 3, 2):
                    g_sent[k, m, f].wait_recv()
                add_dz(at(-m, x) * 2 + (c + f) % 2, False)

    for copy in p_one + q_one + p_two[0] + q_two[0]:
        copy.wait_send()
    for k in (0,) + ORDER:
        for copy in p_two[k] + q_two[k]:
            copy.wait_recv()
    for copy in own_rows:
        copy.wait()

    def through_expert(group):
        rows = fin[group].reshape(256, WIDE)
        gate_col = rows[:, D : D + 1].astype(F32)
        h1 = dot(rows[:, :D], wg[...], 1, 0)
        h2 = dot(rows[:, :D], wu[...], 1, 0)
        here = pl.ds(pl.multiple_of(group * 256, 256), 256)
        dz_here = dz[here, :]
        sigma = jax.nn.sigmoid(h1)
        silu = h1 * sigma
        slope = sigma * (1.0 + h1 * (1.0 - sigma))
        acted = (silu * h2).astype(BF)
        act[here, :] = acted
        gate_grad = jnp.sum(acted.astype(F32) * dz_here, axis=1, keepdims=True)
        pack[group, :, :, D:WIDE] = (
            jnp.broadcast_to(gate_grad, (256, 128)).astype(BF).reshape(4, CAP, 128)
        )
        dfa = gate_col * dz_here
        dhg[here, :] = (dfa * h2 * slope).astype(BF)
        dhu[here, :] = (dfa * silu).astype(BF)

        def back_part(n, _):
            some = pl.ds(pl.multiple_of(n * 512, 512), 512)
            part = dot(dhg[here, :], wg[some, :], 1, 1) + dot(dhu[here, :], wu[some, :], 1, 1)
            pack[group, :, :, some] = part.astype(BF).reshape(4, CAP, 512)
            return 0

        lax.fori_loop(0, 4, back_part, 0)

    r_one, t_one, r_two, t_two, own_back = {}, {}, {}, {}, []

    def forward_back(step):
        if step < 3:
            r_one[step].wait_recv()
            source = at(-1 - step, z)
            r_two[step] = [
                send(bst1.at[source, at(m, y)], back.at[source, y, first], ydev(m)) for m in ORDER
            ]
            own_back.append(local(bst1.at[source, y], back.at[source, y, first]))
        target = at(1 + step, z)
        for n, k in enumerate(ORDER):
            t_one[step][n].wait_recv()
            source = at(-k, y)
            if step < 3:
                t_two[step].append(
                    send(bst2.at[source, target], back.at[z, source, second], zdev(1 + step))
                )
            else:
                own_back.append(local(bst2.at[source, z], back.at[z, source, second]))

    for step in range(4):
        group = at(1 + step, z)
        through_expert(group)
        if step < 3:
            r_one[step] = send(pack.at[group, :, first], bst1.at[z], zdev(1 + step))
            t_two[step] = [send(pack.at[group, y, second], back.at[z, y, second], zdev(1 + step))]
        else:
            r_two[step] = [
                send(pack.at[z, at(m, y), first], back.at[z, y, first], ydev(m)) for m in ORDER
            ]
            own_back.append(local(pack.at[z, y], back.at[z, y]))
        t_one[step] = [
            send(pack.at[group, at(m, y), second], bst2.at[y, group], ydev(m)) for m in ORDER
        ]
        if step >= 2:
            forward_back(step - 2)

    gate_all = fin[:, :, :, D : D + 1].reshape(SLOTS, 1).astype(F32)

    def down_part(shard, _):
        grads = grecv[shard].reshape(SLOTS, SH).astype(F32)
        scaled = (gate_all * grads).astype(BF)
        columns = pl.ds(pl.multiple_of(shard * SH, SH), SH)
        wd[:, columns] = dot(act[...], scaled, 0, 0).astype(BF)
        return 0

    lax.fori_loop(0, 8, down_part, 0)
    written = [local(wd, out_wd)]
    forward_back(2)

    def in_part(source, outgoing):
        def one(n, _):
            some = pl.ds(pl.multiple_of(n * 256, 256), 256)
            rows = fin[:, :, :, some].reshape(SLOTS, 256)
            outgoing[some, :] = dot(rows, source[...], 0, 0).astype(BF)
            return 0

        lax.fori_loop(0, 8, one, 0)

    in_part(dhg, wg)
    written.append(local(wg, out_wg))
    forward_back(3)
    in_part(dhu, wu)
    written.append(local(wu, out_wu))

    for step in range(4):
        for copy in r_two[step]:
            copy.wait_recv()
        for copy in t_two.get(step, []):
            copy.wait_recv()
    for copy in own_back:
        copy.wait()

    def gather_gates(d, total):
        rows = back[d // 4, d % 4, :, D:WIDE][:, 0:1].astype(F32)
        hot = pmat[pl.ds(pl.multiple_of(d * CAP, CAP), CAP), :].astype(F32)
        value = jnp.sum(hot * rows, axis=0, keepdims=True)
        wanted = (d * 8 + col).astype(F32)
        return total + jnp.where(slots[row] == wanted, value, 0.0)

    gsend[...] = lax.fori_loop(0, 16, gather_gates, jnp.zeros((8, TOK), F32))
    grecv_gates[col] = gsend[...]
    gate_sent = []
    for m in (0, 1, 3, 2):
        for f in range(2):
            if (m, f) != (0, 0):
                gate_sent.append(send(gsend, grecv_gates.at[col], xdev(m, f)))

    for copies in g_sent.values():
        copies.wait_send()

    def combine(shard):
        columns = pl.ds(pl.multiple_of(shard * SH, SH), SH)
        return dot(pmat[...], back[:, :, :, columns].reshape(SLOTS, SH), 0, 0)

    to_core = []
    for k in (1, 3, 2, 0):
        shard = at(k, x) * 2 + 1 - c
        gpack[shard, :, 0:2] = combine(shard).astype(BF).reshape(4, 2, CAP, SH)
        to_core.append(send(gpack.at[shard, :, 0:2], core_in.at[at(k, x)], xdev(0, 1)))
    to_x = []
    total = None
    for n, k in enumerate((1, 3, 2, 0)):
        shard = at(k, x) * 2 + c
        part = combine(shard)
        to_core[n].wait_recv()
        part = part + core_in[at(k, x)].reshape(TOK, SH).astype(F32)
        if k:
            gpack[shard, :, 0:2] = part.astype(BF).reshape(4, 2, CAP, SH)
            to_x.append(send(gpack.at[shard, :, 0:2], rs_in.at[x], xdev(k, 0)))
        else:
            total = part
    for n, k in enumerate(ORDER):
        to_x[n].wait_recv()
        total = total + rs_in[at(-k, x)].reshape(TOK, SH).astype(F32)
    out_in[...] = total.astype(BF)

    for copy in gate_sent:
        copy.wait_recv()
    out_gates[...] = jnp.sum(grecv_gates[...], axis=0)

    for copy in x_own + x_core + a_one + b_one + s_one + s_two + gate_sent + to_core + to_x:
        copy.wait_send()
    for k in (0,) + ORDER:
        for copy in a_two[k] + b_two[k]:
            copy.wait_send()
    for k in ORDER:
        for copy in p_two[k] + q_two[k]:
            copy.wait_send()
    for step in range(4):
        if step < 3:
            r_one[step].wait_send()
        for copy in t_one[step] + r_two[step] + t_two.get(step, []):
            copy.wait_send()
    for copy in written:
        copy.wait()


def body(inputs, grad_output, gates, expert_ids, owner, w_gate, w_up, w_down):
    vmem, anywhere = pl.BlockSpec(memory_space=pltpu.VMEM), pl.BlockSpec(memory_space=pl.ANY)
    scratch = [
        ((8, TOK, SH), BF),
        ((16, TOK, SH), BF),
        ((16, 8, TOK), F32),
        ((8, 4, 4, CAP, SH), BF),
        ((8, 4, 4, CAP, SH), BF),
        ((4, 4, CAP, WIDE), BF),
        ((4, 4, HALF, WIDE), BF),
        ((4, 4, HALF, WIDE), BF),
        ((4, 4, CAP, WIDE), BF),
        ((D, FF), BF),
        ((D, FF), BF),
        ((FF, D), BF),
        ((SLOTS, FF), F32),
        ((SLOTS, FF), BF),
        ((SLOTS, FF), BF),
        ((SLOTS, FF), BF),
        ((4, 4, HALF, WIDE), BF),
        ((4, 4, HALF, WIDE), BF),
        ((4, 4, CAP, WIDE), BF),
        ((SLOTS, TOK), BF),
        ((TOK, TOK), BF),
        ((128, TOK), F32),
        ((TOK, TOK), BF),
        ((4, 4, 2, CAP, SH), BF),
        ((4, 4, 2, CAP, SH), BF),
        ((8, TOK), F32),
        ((8, 8, TOK), F32),
    ]
    grad_inputs, grad_gates, grad_gate, grad_up, grad_down = pl.pallas_call(
        kernel,
        out_shape=[
            jax.ShapeDtypeStruct((TOK, SH), BF),
            jax.ShapeDtypeStruct((TOP, TOK), F32),
            jax.ShapeDtypeStruct((D, FF), BF),
            jax.ShapeDtypeStruct((D, FF), BF),
            jax.ShapeDtypeStruct((FF, D), BF),
        ],
        in_specs=[anywhere, anywhere, vmem, vmem, vmem, anywhere, anywhere, anywhere],
        out_specs=[vmem, vmem, anywhere, anywhere, anywhere],
        scratch_shapes=[pltpu.VMEM(shape, kind) for shape, kind in scratch]
        + [
            pltpu.SemaphoreType.DMA((SEMS,)),
            pltpu.SemaphoreType.DMA((SEMS,)),
            pltpu.SemaphoreType.DMA((SEMS // 4,)),
        ],
        compiler_params=pltpu.CompilerParams(
            collective_id=0, has_side_effects=True, vmem_limit_bytes=63 << 20
        ),
    )(
        inputs,
        grad_output,
        expert_ids.T,
        gates.T,
        owner.reshape(1, -1),
        w_gate[0],
        w_up[0],
        w_down[0],
    )
    return (
        grad_inputs,
        grad_gates.T.astype(BF),
        grad_gate[None],
        grad_up[None],
        grad_down[None],
    )


def solution(mesh):
    in_specs = (
        P("dp", "expert"),
        P("dp", "expert"),
        P("dp", None),
        P("dp", None),
        P(),
        P(("dp", "expert"), None, None),
        P(("dp", "expert"), None, None),
        P(("dp", "expert"), None, None),
    )
    out_specs = (
        P("dp", "expert"),
        P("dp", None),
        P(("dp", "expert"), None, None),
        P(("dp", "expert"), None, None),
        P(("dp", "expert"), None, None),
    )
    return jax.shard_map(body, mesh=mesh, in_specs=in_specs, out_specs=out_specs, check_vma=False)
```

```python
import jax
import jax.numpy as jnp
from jax import lax
from jax.experimental import pallas as pl
from jax.experimental.pallas import tpu as pltpu
from jax.sharding import PartitionSpec as P

D, FF, TOP, TOK, CAP = 2048, 768, 8, 512, 64
HALF = CAP // 2
SH = 256
WIDE = D + 128
SLOTS = 1024
SEMS = 160
BF, F32 = jnp.bfloat16, jnp.float32
MESH = pl.DeviceIdType.MESH
ORDER = (1, 3, 2)


def dot(left, right, dim_left, dim_right):
    return lax.dot_general(
        left, right, (((dim_left,), (dim_right,)), ((), ())), preferred_element_type=F32
    )


def iota(shape, dim):
    return lax.broadcasted_iota(jnp.int32, shape, dim).astype(F32)


def kernel(
    inp, gro, ids, gates, owner, wg_in, wu_in, wd_in,
    out_in, out_gates, wg, wu, wd,
    xin, ag, slots, gpack, grecv, pack, st1, st2, fin, dz, act, dhg, dhu,
    bst1, bst2, back, pmat, pmat_t, tri, rall, onehot, core_in, rs_in, gsend, grecv_gates,
    send_sem, recv_sem, local_sem,
):
    row, col = lax.axis_index("dp"), lax.axis_index("expert")
    z, y = row // 4, row % 4
    x, c = col // 2, col % 2
    counts = {"remote": 0, "local": 0}

    def at(k, base):
        return (base + k + 4) % 4

    def zdev(k):
        return (at(k, z) * 4 + y, col)

    def ydev(k):
        return (z * 4 + at(k, y), col)

    def xdev(k, flip):
        return (row, at(k, x) * 2 + (c + flip) % 2)

    def send(src, dst, device):
        n = counts["remote"]
        counts["remote"] = n + 1
        copy = pltpu.make_async_remote_copy(
            src_ref=src, dst_ref=dst, send_sem=send_sem.at[n], recv_sem=recv_sem.at[n],
            device_id=device, device_id_type=MESH,
        )
        copy.start()
        return copy

    def local(src, dst):
        n = counts["local"]
        counts["local"] = n + 1
        copy = pltpu.make_async_copy(src, dst, local_sem.at[n])
        copy.start()
        return copy

    def arrive(label, copies):
        for copy in copies:
            copy.wait_recv()

    def leave(label, copies):
        for copy in copies:
            copy.wait_send()

    def done(label, copies):
        for copy in copies:
            copy.wait()

    weights = [local(wg_in, wg), local(wu_in, wu), local(wd_in, wd)]
    own_in, own_gro = local(inp, xin.at[col]), local(gro, ag.at[row])

    barrier = pltpu.get_barrier_semaphore()
    peers = [zdev(k) for k in ORDER] + [ydev(k) for k in ORDER]
    peers += [xdev(k, f) for k in range(4) for f in range(2) if (k, f) != (0, 0)]
    for peer in peers:
        pl.semaphore_signal(barrier, inc=1, device_id=peer, device_id_type=MESH)
    pl.semaphore_wait(barrier, len(peers))

    x_own = [send(inp, xin.at[col], xdev(k, 0)) for k in ORDER]
    x_core = [send(inp, xin.at[col], xdev(0, 1))]
    lower, upper = pl.ds(0, TOK // 2), pl.ds(TOK // 2, TOK // 2)
    a_one = [send(gro.at[lower], ag.at[row, lower], ydev(k)) for k in ORDER]
    b_one = [send(gro.at[upper], ag.at[row, upper], zdev(k)) for k in ORDER]
    a_two = {0: [send(gro.at[lower], ag.at[row, lower], zdev(k)) for k in ORDER]}
    b_two = {0: [send(gro.at[upper], ag.at[row, upper], ydev(k)) for k in ORDER]}

    tri[...] = (iota((TOK, TOK), 0) <= iota((TOK, TOK), 1)).astype(BF)
    expert_no = lax.broadcasted_iota(jnp.int32, (128, TOK), 0)
    owner_row = jnp.broadcast_to(owner[...].astype(F32), (8, 128)).astype(BF)
    for k in range(TOP):
        match = (ids[k : k + 1, :] == expert_no).astype(F32).astype(BF)
        slots[row, k : k + 1, :] = dot(owner_row, match, 1, 0)[0:1, :]
    s_one = [send(slots.at[row], slots.at[row], ydev(k)) for k in ORDER]

    mine = slots[row]
    name = iota((16, TOK), 0) * 8.0 + col.astype(F32)
    member = jnp.zeros((16, TOK), F32)
    gate_of = jnp.zeros((16, TOK), F32)
    for k in range(TOP):
        hit = mine[k : k + 1, :] == name
        member += jnp.where(hit, 1.0, 0.0)
        gate_of += jnp.where(hit, gates[k : k + 1, :].astype(F32), 0.0)
    rank = dot(member.astype(BF), tri[...], 1, 0) * member
    place = iota((CAP, TOK), 0) + 1.0
    for d in range(16):
        hot = jnp.where(rank[d : d + 1, :] == place, 1.0, 0.0)
        pmat[d * CAP : (d + 1) * CAP, :] = hot.astype(BF)
        gate_col = jnp.sum(hot * gate_of[d : d + 1, :], axis=1, keepdims=True)
        pack[d // 4, d % 4, :, D:WIDE] = jnp.broadcast_to(gate_col, (CAP, 128)).astype(BF)

    arrive("slots", s_one)
    s_two = [
        send(slots.at[pl.ds(z * 4, 4)], slots.at[pl.ds(z * 4, 4)], zdev(k)) for k in ORDER
    ]
    for n, k in enumerate(ORDER):
        arrive("x_own", [x_own[n]])
        source = at(-k, x) * 2 + c
        x_core.append(send(xin.at[source], xin.at[source], xdev(0, 1)))
        arrive("a_one", [a_one[n]])
        source = z * 4 + at(-k, y)
        a_two[k] = [
            send(ag.at[source, lower], ag.at[source, lower], zdev(m)) for m in ORDER
        ]
        arrive("b_one", [b_one[n]])
        source = at(-k, z) * 4 + y
        b_two[k] = [
            send(ag.at[source, upper], ag.at[source, upper], ydev(m)) for m in ORDER
        ]

    near = iota((8, TOK), 0) + row.astype(F32) * 8.0

    def rank_members(group):
        def one(step, _):
            found = jnp.zeros((8, TOK), F32)
            theirs = slots[group * 4 + step]
            for k in range(TOP):
                found += jnp.where(theirs[k : k + 1, :] == near, 1.0, 0.0)
            rall[pl.ds(pl.multiple_of(step * 8, 8), 8), :] = found
            return 0

        lax.fori_loop(0, 4, one, 0)
        rall[...] = dot(rall[...].astype(BF), tri[...], 1, 0) * rall[...]

    def pack_gradients(group):
        rank_members(group)

        def one(step, _):
            r = group * 4 + step
            ranks = rall[pl.ds(pl.multiple_of(step * 8, 8), 8), :]
            for e in range(8):
                hot = jnp.where(ranks[e : e + 1, :] == place, 1.0, 0.0)
                onehot[e * CAP : (e + 1) * CAP, :] = hot.astype(BF)
            rows = dot(onehot[...], ag[r], 1, 0).astype(BF)
            gpack[:, group, step] = rows.reshape(8, CAP, SH)
            return 0

        lax.fori_loop(0, 4, one, 0)

    g_sent = {}
    own_grads = []

    def exchange_gradients(group, k):
        for m in (0, 1, 3, 2):
            for f in range(2):
                target = at(m, x) * 2 + (c + f) % 2
                if (m, f) == (0, 0):
                    own_grads.append(local(gpack.at[col, group], grecv.at[col, group]))
                else:
                    g_sent[k, m, f] = send(
                        gpack.at[target, group], grecv.at[col, group], xdev(m, f)
                    )

    arrive("b_two", b_two[0])
    own_gro.wait()
    pack_gradients(z)
    exchange_gradients(z, 0)

    arrive("x_core", x_core)
    own_in.wait()

    def pack_inputs(shard, _):
        rows = dot(pmat[...], xin[shard], 1, 0).astype(BF)
        pack[:, :, :, pl.ds(pl.multiple_of(shard * SH, SH), SH)] = rows.reshape(4, 4, CAP, SH)
        return 0

    lax.fori_loop(0, 8, pack_inputs, 0)

    first, second = pl.ds(0, HALF), pl.ds(HALF, HALF)
    p_one = [send(pack.at[:, at(k, y), first], st1.at[y], ydev(k)) for k in ORDER]
    q_one = [send(pack.at[at(k, z), :, second], st2.at[z], zdev(k)) for k in ORDER]
    p_two = {0: [send(pack.at[at(k, z), y, first], fin.at[z, y, first], zdev(k)) for k in ORDER]}
    q_two = {0: [send(pack.at[z, at(k, y), second], fin.at[z, y, second], ydev(k)) for k in ORDER]}
    own_rows = [local(pack.at[z, y], fin.at[z, y])]

    arrive("slots_two", s_two)
    for n, k in enumerate(ORDER):
        arrive("b_two", b_two[k])
        arrive("a_two", [a_two[source][n] for source in (0, 1, 3, 2)])
        group = at(-k, z)
        pack_gradients(group)
        exchange_gradients(group, k)

    for n, k in enumerate(ORDER):
        arrive("p_one", [p_one[n]])
        source = at(-k, y)
        p_two[k] = [
            send(st1.at[source, at(m, z)], fin.at[z, source, first], zdev(m)) for m in ORDER
        ]
        own_rows.append(local(st1.at[source, z], fin.at[z, source, first]))
        arrive("q_one", [q_one[n]])
        source = at(-k, z)
        q_two[k] = [
            send(st2.at[source, at(m, y)], fin.at[source, y, second], ydev(m)) for m in ORDER
        ]
        own_rows.append(local(st2.at[source, y], fin.at[source, y, second]))

    pmat_t[...] = pmat[...].T

    done("weights", weights + own_grads)

    def add_dz(shard, start):
        columns = pl.ds(pl.multiple_of(shard * SH, SH), SH)

        def chunk(n, _):
            rows = pl.ds(pl.multiple_of(n * 256, 256), 256)
            part = dot(grecv[shard, n].reshape(256, SH), wd[:, columns], 1, 1)
            dz[rows, :] = part if start else dz[rows, :] + part
            return 0

        lax.fori_loop(0, 4, chunk, 0)

    add_dz(col, True)
    for m in (0, 1, 3, 2):
        for f in range(2):
            if (m, f) != (0, 0):
                arrive("grads", [g_sent[k, m, f] for k in (0, 1, 3, 2)])
                add_dz(at(-m, x) * 2 + (c + f) % 2, False)

    leave("pack", p_one + q_one + p_two[0] + q_two[0])
    for k in (0,) + ORDER:
        arrive("rows", p_two[k] + q_two[k])
    done("own_rows", own_rows)

    def through_expert(group):
        rows = fin[group].reshape(256, WIDE)
        gate_col = rows[:, D : D + 1].astype(F32)
        h1 = dot(rows[:, :D], wg[...], 1, 0)
        h2 = dot(rows[:, :D], wu[...], 1, 0)
        here = pl.ds(pl.multiple_of(group * 256, 256), 256)
        dz_here = dz[here, :]
        sigma = jax.nn.sigmoid(h1)
        silu = h1 * sigma
        slope = sigma * (1.0 + h1 * (1.0 - sigma))
        acted = (silu * h2).astype(BF)
        act[here, :] = acted
        gate_grad = jnp.sum(acted.astype(F32) * dz_here, axis=1, keepdims=True)
        pack[group, :, :, D:WIDE] = (
            jnp.broadcast_to(gate_grad, (256, 128)).astype(BF).reshape(4, CAP, 128)
        )
        dfa = gate_col * dz_here
        dhg[here, :] = (dfa * h2 * slope).astype(BF)
        dhu[here, :] = (dfa * silu).astype(BF)

        def back_part(n, _):
            some = pl.ds(pl.multiple_of(n * 512, 512), 512)
            part = dot(dhg[here, :], wg[some, :], 1, 1) + dot(dhu[here, :], wu[some, :], 1, 1)
            pack[group, :, :, some] = part.astype(BF).reshape(4, CAP, 512)
            return 0

        lax.fori_loop(0, 4, back_part, 0)

    r_one, t_one, r_two, t_two, own_back = {}, {}, {}, {}, []

    def forward_back(step):
        if step < 3:
            arrive("r_one", [r_one[step]])
            source = at(-1 - step, z)
            r_two[step] = [
                send(bst1.at[source, at(m, y)], back.at[source, y, first], ydev(m)) for m in ORDER
            ]
            own_back.append(local(bst1.at[source, y], back.at[source, y, first]))
        target = at(1 + step, z)
        for n, k in enumerate(ORDER):
            arrive("t_one", [t_one[step][n]])
            source = at(-k, y)
            if step < 3:
                t_two[step].append(
                    send(bst2.at[source, target], back.at[z, source, second], zdev(1 + step))
                )
            else:
                own_back.append(local(bst2.at[source, z], back.at[z, source, second]))

    for step in range(4):
        group = at(1 + step, z)
        through_expert(group)
        if step < 3:
            r_one[step] = send(pack.at[group, :, first], bst1.at[z], zdev(1 + step))
            t_two[step] = [send(pack.at[group, y, second], back.at[z, y, second], zdev(1 + step))]
        else:
            r_two[step] = [
                send(pack.at[z, at(m, y), first], back.at[z, y, first], ydev(m)) for m in ORDER
            ]
            own_back.append(local(pack.at[z, y], back.at[z, y]))
        t_one[step] = [
            send(pack.at[group, at(m, y), second], bst2.at[y, group], ydev(m)) for m in ORDER
        ]
        if step >= 2:
            forward_back(step - 2)

    gate_all = fin[:, :, :, D : D + 1].reshape(SLOTS, 1).astype(F32)

    def down_part(shard, _):
        grads = grecv[shard].reshape(SLOTS, SH).astype(F32)
        scaled = (gate_all * grads).astype(BF)
        columns = pl.ds(pl.multiple_of(shard * SH, SH), SH)
        wd[:, columns] = dot(act[...], scaled, 0, 0).astype(BF)
        return 0

    lax.fori_loop(0, 8, down_part, 0)
    forward_back(2)

    def in_part(source, outgoing):
        def one(n, _):
            some = pl.ds(pl.multiple_of(n * 256, 256), 256)
            rows = fin[:, :, :, some].reshape(SLOTS, 256)
            outgoing[some, :] = dot(rows, source[...], 0, 0).astype(BF)
            return 0

        lax.fori_loop(0, 8, one, 0)

    in_part(dhg, wg)
    forward_back(3)
    in_part(dhu, wu)

    for step in range(4):
        arrive("r_two", r_two[step])
        arrive("t_two", t_two.get(step, []))
    done("own_back", own_back)

    slot_no = lax.broadcasted_iota(jnp.int32, (SLOTS, 128), 0) // CAP
    in_place = slot_no == lax.broadcasted_iota(jnp.int32, (SLOTS, 128), 1)
    spread = jnp.where(in_place, back[:, :, :, D:WIDE].reshape(SLOTS, 128).astype(F32), 0.0)
    values = dot(pmat_t[...], spread.astype(BF), 1, 0).T
    total_gates = jnp.zeros((TOP, TOK), F32)
    for d in range(16):
        wanted = (col + d * 8).astype(F32)
        total_gates += jnp.where(mine == wanted, values[d : d + 1, :], 0.0)
    gsend[...] = total_gates
    grecv_gates[col] = gsend[...]
    gate_sent = []
    for m in (0, 1, 3, 2):
        for f in range(2):
            if (m, f) != (0, 0):
                gate_sent.append(send(gsend, grecv_gates.at[col], xdev(m, f)))

    leave("g_sent", g_sent.values())

    def combine(shard):
        columns = pl.ds(pl.multiple_of(shard * SH, SH), SH)
        return dot(pmat_t[...], back[:, :, :, columns].reshape(SLOTS, SH), 1, 0)

    to_core = []
    for k in (1, 3, 2, 0):
        shard = at(k, x) * 2 + 1 - c
        gpack[shard, :, 0:2] = combine(shard).astype(BF).reshape(4, 2, CAP, SH)
        to_core.append(send(gpack.at[shard, :, 0:2], core_in.at[at(k, x)], xdev(0, 1)))
    to_x = []
    total = None
    for n, k in enumerate((1, 3, 2, 0)):
        shard = at(k, x) * 2 + c
        part = combine(shard)
        arrive("to_core", [to_core[n]])
        part = part + core_in[at(k, x)].reshape(TOK, SH).astype(F32)
        if k:
            gpack[shard, :, 0:2] = part.astype(BF).reshape(4, 2, CAP, SH)
            to_x.append(send(gpack.at[shard, :, 0:2], rs_in.at[x], xdev(k, 0)))
        else:
            total = part
    for n, k in enumerate(ORDER):
        arrive("to_x", [to_x[n]])
        total = total + rs_in[at(-k, x)].reshape(TOK, SH).astype(F32)
    out_in[...] = total.astype(BF)

    arrive("gate_sent", gate_sent)
    out_gates[...] = jnp.sum(grecv_gates[...], axis=0).astype(BF)

    leave("first", x_own + x_core + a_one + b_one + s_one + s_two)
    for k in (0,) + ORDER:
        leave("gather", a_two[k] + b_two[k])
    for k in ORDER:
        leave("rows", p_two[k] + q_two[k])
    for step in range(4):
        leave("back", t_one[step] + r_two[step] + t_two.get(step, []))
    leave("back", r_one.values())
    leave("sums", gate_sent + to_core + to_x)


def write_out(*refs):
    sem = refs[10]
    copies = [pltpu.make_async_copy(refs[n], refs[5 + n], sem.at[n]) for n in range(5)]
    for copy in copies:
        copy.start()
    for copy in copies:
        copy.wait()


def body(inputs, grad_output, gates, expert_ids, owner, w_gate, w_up, w_down):
    vmem, anywhere = pl.BlockSpec(memory_space=pltpu.VMEM), pl.BlockSpec(memory_space=pl.ANY)
    scratch = [
        ((8, TOK, SH), BF),
        ((16, TOK, SH), BF),
        ((16, 8, TOK), F32),
        ((8, 4, 4, CAP, SH), BF),
        ((8, 4, 4, CAP, SH), BF),
        ((4, 4, CAP, WIDE), BF),
        ((4, 4, HALF, WIDE), BF),
        ((4, 4, HALF, WIDE), BF),
        ((4, 4, CAP, WIDE), BF),
        ((SLOTS, FF), F32),
        ((SLOTS, FF), BF),
        ((SLOTS, FF), BF),
        ((SLOTS, FF), BF),
        ((4, 4, HALF, WIDE), BF),
        ((4, 4, HALF, WIDE), BF),
        ((4, 4, CAP, WIDE), BF),
        ((SLOTS, TOK), BF),
        ((TOK, SLOTS), BF),
        ((TOK, TOK), BF),
        ((32, TOK), F32),
        ((TOK, TOK), BF),
        ((4, 4, 2, CAP, SH), BF),
        ((4, 4, 2, CAP, SH), BF),
        ((8, TOK), F32),
        ((8, 8, TOK), F32),
    ]
    results = [
        ((TOK, SH), BF),
        ((TOP, TOK), BF),
        ((D, FF), BF),
        ((D, FF), BF),
        ((FF, D), BF),
    ]
    held = pl.pallas_call(
        kernel,
        out_shape=[pltpu.VMEM(shape, kind) for shape, kind in results],
        in_specs=[anywhere, anywhere, vmem, vmem, vmem, anywhere, anywhere, anywhere],
        out_specs=[vmem] * 5,
        scratch_shapes=[pltpu.VMEM(shape, kind) for shape, kind in scratch]
        + [
            pltpu.SemaphoreType.DMA((SEMS,)),
            pltpu.SemaphoreType.DMA((SEMS,)),
            pltpu.SemaphoreType.DMA((SEMS // 4,)),
        ],
        compiler_params=pltpu.CompilerParams(
            collective_id=0, has_side_effects=True, vmem_limit_bytes=53 << 20
        ),
    )(
        inputs,
        grad_output,
        expert_ids.T,
        gates.T,
        owner.reshape(1, -1),
        w_gate[0],
        w_up[0],
        w_down[0],
    )
    grad_inputs, grad_gates, grad_gate, grad_up, grad_down = pl.pallas_call(
        write_out,
        out_shape=[jax.ShapeDtypeStruct(shape, kind) for shape, kind in results],
        in_specs=[vmem] * 5,
        out_specs=[anywhere] * 5,
        scratch_shapes=[pltpu.SemaphoreType.DMA((5,))],
        compiler_params=pltpu.CompilerParams(vmem_limit_bytes=16 << 20),
    )(*[pltpu.with_memory_space_constraint(array, pltpu.VMEM) for array in held])
    return (
        grad_inputs,
        grad_gates.T,
        grad_gate[None],
        grad_up[None],
        grad_down[None],
    )


def solution(mesh):
    in_specs = (
        P("dp", "expert"),
        P("dp", "expert"),
        P("dp", None),
        P("dp", None),
        P(),
        P(("dp", "expert"), None, None),
        P(("dp", "expert"), None, None),
        P(("dp", "expert"), None, None),
    )
    out_specs = (
        P("dp", "expert"),
        P("dp", None),
        P(("dp", "expert"), None, None),
        P(("dp", "expert"), None, None),
        P(("dp", "expert"), None, None),
    )
    return jax.shard_map(body, mesh=mesh, in_specs=in_specs, out_specs=out_specs, check_vma=False)
```

```python
import jax
import jax.numpy as jnp
from jax import lax
from jax.experimental import pallas as pl
from jax.experimental.pallas import tpu as pltpu
from jax.sharding import PartitionSpec as P

D, FF, TOP, TOK, CAP = 2048, 768, 8, 512, 64
HALF = CAP // 2
SH = 256
WIDE = D + 128
SLOTS = 1024
SEMS = 192
BF, F32 = jnp.bfloat16, jnp.float32
MESH = pl.DeviceIdType.MESH
ORDER = (1, 3, 2)


def dot(left, right, dim_left, dim_right):
    return lax.dot_general(
        left, right, (((dim_left,), (dim_right,)), ((), ())), preferred_element_type=F32
    )


def iota(shape, dim):
    return lax.broadcasted_iota(jnp.int32, shape, dim).astype(F32)


def kernel(
    inp, gro, ids, gates, owner, wg_in, wu_in, wd_in,
    out_in, out_gates, wg, wu, wd,
    xin, ag, slots, gpack, grecv, pack, st1, st2, fin, dz, act, dhg, dhu, some_g, some_u,
    bst1, bst2, back, pmat, pmat_t, tri, rall, onehot, gsend, grecv_gates,
    send_sem, recv_sem, local_sem,
):
    row, col = lax.axis_index("dp"), lax.axis_index("expert")
    z, y = row // 4, row % 4
    x, c = col // 2, col % 2
    counts = {"remote": 0, "local": 0}

    def at(k, base):
        return (base + k + 4) % 4

    def zdev(k):
        return (at(k, z) * 4 + y, col)

    def ydev(k):
        return (z * 4 + at(k, y), col)

    def xdev(k, flip):
        return (row, at(k, x) * 2 + (c + flip) % 2)

    def send(src, dst, device):
        n = counts["remote"]
        counts["remote"] = n + 1
        copy = pltpu.make_async_remote_copy(
            src_ref=src, dst_ref=dst, send_sem=send_sem.at[n], recv_sem=recv_sem.at[n],
            device_id=device, device_id_type=MESH,
        )
        copy.start()
        return copy

    def local(src, dst):
        n = counts["local"]
        counts["local"] = n + 1
        copy = pltpu.make_async_copy(src, dst, local_sem.at[n])
        copy.start()
        return copy

    def arrive(label, copies):
        for copy in copies:
            copy.wait_recv()

    def leave(label, copies):
        for copy in copies:
            copy.wait_send()

    def done(label, copies):
        for copy in copies:
            copy.wait()

    weights = [local(wg_in, wg), local(wu_in, wu), local(wd_in, wd)]
    own_in, own_gro = local(inp, xin.at[col]), local(gro, ag.at[row])

    barrier = pltpu.get_barrier_semaphore()
    peers = [zdev(k) for k in ORDER] + [ydev(k) for k in ORDER]
    peers += [xdev(k, f) for k in range(4) for f in range(2) if (k, f) != (0, 0)]
    for peer in peers:
        pl.semaphore_signal(barrier, inc=1, device_id=peer, device_id_type=MESH)
    pl.semaphore_wait(barrier, len(peers))

    x_own = [send(inp, xin.at[col], xdev(k, 0)) for k in ORDER]
    x_core = [send(inp, xin.at[col], xdev(0, 1))]
    def half(path):
        return pl.ds(path * 256, 256)

    def quarter(path, n):
        return pl.ds(path * 256 + n * 128, 128)

    def along(path, stage, k):
        return ydev(k) if path == stage - 1 else zdev(k)

    def row_at(path, near, far):
        if path == 0:
            return at(far, z) * 4 + at(near, y)
        return at(near, z) * 4 + at(far, y)

    both = (1, -1)
    one, two, one_on, two_on = {}, {}, {}, {}
    for path in range(2):
        for k in both:
            one[path, k] = send(
                gro.at[half(path)], ag.at[row, half(path)], along(path, 1, k)
            )
    for path in range(2):
        for k in both:
            two[path, 0, k] = send(
                gro.at[half(path)], ag.at[row, half(path)], along(path, 2, k)
            )

    def pass_block(path, near):
        here = ag.at[row_at(path, near, 0), half(path)]
        for k in both:
            two[path, near, k] = send(here, here, along(path, 2, k))

    def pass_on(path, stage, near, k):
        source = row_at(path, -k, 0) if stage == 1 else row_at(path, near, -k)
        here = ag.at[source, quarter(path, 0 if k == 1 else 1)]
        return send(here, here, along(path, stage, k))

    tri[...] = (iota((TOK, TOK), 0) <= iota((TOK, TOK), 1)).astype(BF)
    expert_no = lax.broadcasted_iota(jnp.int32, (128, TOK), 0)
    owner_row = jnp.broadcast_to(owner[...].astype(F32), (8, 128)).astype(BF)
    for k in range(TOP):
        match = (ids[k : k + 1, :] == expert_no).astype(F32).astype(BF)
        slots[row, k : k + 1, :] = dot(owner_row, match, 1, 0)[0:1, :]
    s_one = [send(slots.at[row], slots.at[row], ydev(k)) for k in ORDER]

    mine = slots[row]
    name = iota((16, TOK), 0) * 8.0 + col.astype(F32)
    member = jnp.zeros((16, TOK), F32)
    gate_of = jnp.zeros((16, TOK), F32)
    for k in range(TOP):
        hit = mine[k : k + 1, :] == name
        member += jnp.where(hit, 1.0, 0.0)
        gate_of += jnp.where(hit, gates[k : k + 1, :].astype(F32), 0.0)
    rank = dot(member.astype(BF), tri[...], 1, 0) * member
    place = iota((CAP, TOK), 0) + 1.0
    for d in range(16):
        hot = jnp.where(rank[d : d + 1, :] == place, 1.0, 0.0)
        pmat[d * CAP : (d + 1) * CAP, :] = hot.astype(BF)
        gate_col = jnp.sum(hot * gate_of[d : d + 1, :], axis=1, keepdims=True)
        pack[d // 4, d % 4, :, D:WIDE] = jnp.broadcast_to(gate_col, (CAP, 128)).astype(BF)

    arrive("slots", s_one)
    s_two = [
        send(slots.at[pl.ds(z * 4, 4)], slots.at[pl.ds(z * 4, 4)], zdev(k)) for k in ORDER
    ]

    neighbours = iota((8, TOK), 0) + row.astype(F32) * 8.0

    def rank_members(group):
        def one(step, _):
            found = jnp.zeros((8, TOK), F32)
            theirs = slots[group * 4 + step]
            for k in range(TOP):
                found += jnp.where(theirs[k : k + 1, :] == neighbours, 1.0, 0.0)
            rall[pl.ds(pl.multiple_of(step * 8, 8), 8), :] = found
            return 0

        lax.fori_loop(0, 4, one, 0)
        rall[...] = dot(rall[...].astype(BF), tri[...], 1, 0) * rall[...]

    def pack_gradients(group):
        rank_members(group)

        def one(step, _):
            r = group * 4 + step
            ranks = rall[pl.ds(pl.multiple_of(step * 8, 8), 8), :]
            for e in range(8):
                hot = jnp.where(ranks[e : e + 1, :] == place, 1.0, 0.0)
                onehot[e * CAP : (e + 1) * CAP, :] = hot.astype(BF)
            rows = dot(onehot[...], ag[r], 1, 0).astype(BF)
            gpack[:, group, step] = rows.reshape(8, CAP, SH)
            return 0

        lax.fori_loop(0, 4, one, 0)

    g_sent = {}
    own_grads = []

    def exchange_gradients(group, k):
        for m in (0, 1, 3, 2):
            for f in range(2):
                target = at(m, x) * 2 + (c + f) % 2
                if (m, f) == (0, 0):
                    own_grads.append(local(gpack.at[col, group], grecv.at[col, group]))
                else:
                    g_sent[k, m, f] = send(
                        gpack.at[target, group], grecv.at[col, group], xdev(m, f)
                    )

    for path in range(2):
        for k in both:
            arrive("one", [one[path, k]])
            one_on[path, k] = pass_on(path, 1, 0, k)
            pass_block(path, -k)
    for path in range(2):
        for k in both:
            arrive("two", [two[path, 0, k]])
            two_on[path, 0, k] = pass_on(path, 2, 0, k)
    for path in range(2):
        arrive("one_on", [one_on[path, k] for k in both])
        pass_block(path, 2)
    for n, k in enumerate(ORDER):
        arrive("x_own", [x_own[n]])
        source = at(-k, x) * 2 + c
        x_core.append(send(xin.at[source], xin.at[source], xdev(0, 1)))

    def pass_far(near):
        for path in range(2):
            for k in both:
                arrive("two", [two[path, near, k]])
                two_on[path, near, k] = pass_on(path, 2, near, k)

    arrive("two_on", [two_on[1, 0, k] for k in both])
    own_gro.wait()
    pack_gradients(z)
    exchange_gradients(z, 0)

    pass_far(-1)

    arrive("x_core", x_core)
    own_in.wait()

    def pack_inputs(shard, _):
        rows = dot(pmat[...], xin[shard], 1, 0).astype(BF)
        pack[:, :, :, pl.ds(pl.multiple_of(shard * SH, SH), SH)] = rows.reshape(4, 4, CAP, SH)
        return 0

    lax.fori_loop(0, 8, pack_inputs, 0)

    first, second = pl.ds(0, HALF), pl.ds(HALF, HALF)
    p_two = {0: [send(pack.at[at(k, z), y, first], fin.at[z, y, first], zdev(k)) for k in ORDER]}
    q_two = {0: [send(pack.at[z, at(k, y), second], fin.at[z, y, second], ydev(k)) for k in ORDER]}
    own_rows = [local(pack.at[z, y], fin.at[z, y])]

    pass_far(1)
    pass_far(2)
    p_one = [send(pack.at[:, at(k, y), first], st1.at[y], ydev(k)) for k in ORDER]
    q_one = [send(pack.at[at(k, z), :, second], st2.at[z], zdev(k)) for k in ORDER]

    leave("x_core", x_core)
    arrive("slots_two", s_two)
    for k, near in zip(ORDER, (-1, 1, 2)):
        arrive("two_on", [two_on[1, near, m] for m in both])
        if k == 2:
            arrive("two_on", [two_on[0, n, m] for n in (0, -1, 1, 2) for m in both])
        group = at(-k, z)
        pack_gradients(group)
        exchange_gradients(group, k)

    for n, k in enumerate(ORDER):
        arrive("p_one", [p_one[n]])
        source = at(-k, y)
        p_two[k] = [
            send(st1.at[source, at(m, z)], fin.at[z, source, first], zdev(m)) for m in ORDER
        ]
        own_rows.append(local(st1.at[source, z], fin.at[z, source, first]))
        arrive("q_one", [q_one[n]])
        source = at(-k, z)
        q_two[k] = [
            send(st2.at[source, at(m, y)], fin.at[source, y, second], ydev(m)) for m in ORDER
        ]
        own_rows.append(local(st2.at[source, y], fin.at[source, y, second]))

    pmat_t[...] = pmat[...].T

    done("weights", weights + own_grads)

    def add_dz(shard, start):
        columns = pl.ds(pl.multiple_of(shard * SH, SH), SH)

        def chunk(n, _):
            part = dot(grecv[shard, n].reshape(256, SH), wd[:, columns], 1, 1)
            part = part.reshape(4, CAP, FF)
            dz[n] = part if start else dz[n] + part
            return 0

        lax.fori_loop(0, 4, chunk, 0)

    add_dz(col, True)
    for m in (0, 1, 3, 2):
        for f in range(2):
            if (m, f) != (0, 0):
                arrive("grads", [g_sent[k, m, f] for k in (0, 1, 3, 2)])
                add_dz(at(-m, x) * 2 + (c + f) % 2, False)

    leave("pack", p_one + q_one + p_two[0] + q_two[0])
    done("own_rows", own_rows)

    def chunk_of(ref, zk, yk, width):
        lower_rows = ref[zk, :, 0:HALF, 0:width].reshape(4 * HALF, width)
        upper_rows = ref[:, yk, HALF:CAP, 0:width].reshape(4 * HALF, width)
        return jnp.concatenate([lower_rows, upper_rows], axis=0)

    def put_chunk(ref, zk, yk, columns, value):
        width = value.shape[1]
        ref[zk, :, 0:HALF, columns] = value[: 4 * HALF].reshape(4, HALF, width)
        ref[:, yk, HALF:CAP, columns] = value[4 * HALF :].reshape(4, HALF, width)

    def through_expert(zk, yk):
        rows = chunk_of(fin, zk, yk, WIDE)
        gate_col = rows[:, D : D + 1].astype(F32)
        h1 = dot(rows[:, :D], wg[...], 1, 0)
        h2 = dot(rows[:, :D], wu[...], 1, 0)
        dz_here = chunk_of(dz, zk, yk, FF)
        sigma = jax.nn.sigmoid(h1)
        silu = h1 * sigma
        slope = sigma * (1.0 + h1 * (1.0 - sigma))
        acted = (silu * h2).astype(BF)
        every = pl.ds(0, FF)
        put_chunk(act, zk, yk, every, acted)
        gate_grad = jnp.sum(acted.astype(F32) * dz_here, axis=1, keepdims=True)
        put_chunk(pack, zk, yk, pl.ds(D, 128), jnp.broadcast_to(gate_grad, (256, 128)).astype(BF))
        dfa = gate_col * dz_here
        some_g[...] = (dfa * h2 * slope).astype(BF)
        some_u[...] = (dfa * silu).astype(BF)
        put_chunk(dhg, zk, yk, every, some_g[...])
        put_chunk(dhu, zk, yk, every, some_u[...])

        def back_part(n, _):
            some = pl.ds(pl.multiple_of(n * 512, 512), 512)
            part = dot(some_g[...], wg[some, :], 1, 1) + dot(some_u[...], wu[some, :], 1, 1)
            put_chunk(pack, zk, yk, some, part.astype(BF))
            return 0

        lax.fori_loop(0, 4, back_part, 0)

    r_one, t_one, r_two, t_two, own_back = {}, {}, {}, {}, []

    def forward_back(k):
        arrive("r_one", [r_one[k]])
        source = at(k, z)
        r_two[k] = [
            send(bst1.at[source, at(m, y)], back.at[source, y, first], ydev(m)) for m in ORDER
        ]
        own_back.append(local(bst1.at[source, y], back.at[source, y, first]))
        arrive("t_one", [t_one[k]])
        source = at(k, y)
        t_two[k] = [
            send(bst2.at[source, at(m, z)], back.at[z, source, second], zdev(m)) for m in ORDER
        ]
        own_back.append(local(bst2.at[source, z], back.at[z, source, second]))

    for k in (0,) + ORDER:
        zk, yk = at(-k, z), at(-k, y)
        if k:
            n = ORDER.index(k)
            arrive("rows", [p_two[source][n] for source in (0, 1, 3, 2)])
            arrive("rows", [q_two[source][n] for source in (0, 1, 3, 2)])
        through_expert(zk, yk)
        if k:
            r_one[k] = send(pack.at[zk, :, first], bst1.at[z], zdev(-k))
            t_one[k] = send(pack.at[:, yk, second], bst2.at[y], ydev(-k))
        else:
            r_two[0] = [
                send(pack.at[z, at(m, y), first], back.at[z, y, first], ydev(m)) for m in ORDER
            ]
            t_two[0] = [
                send(pack.at[at(m, z), y, second], back.at[z, y, second], zdev(m)) for m in ORDER
            ]
            own_back.append(local(pack.at[z, y], back.at[z, y]))

    gate_all = fin[:, :, :, D : D + 1].reshape(SLOTS, 1).astype(F32)

    def down_part(shard, _):
        grads = grecv[shard].reshape(SLOTS, SH).astype(F32)
        scaled = (gate_all * grads).astype(BF)
        columns = pl.ds(pl.multiple_of(shard * SH, SH), SH)
        wd[:, columns] = dot(act[...].reshape(SLOTS, FF), scaled, 0, 0).astype(BF)
        return 0

    lax.fori_loop(0, 4, down_part, 0)
    forward_back(1)
    lax.fori_loop(4, 8, down_part, 0)
    forward_back(3)

    def in_part(source, outgoing):
        def one(n, _):
            some = pl.ds(pl.multiple_of(n * 256, 256), 256)
            rows = fin[:, :, :, some].reshape(SLOTS, 256)
            outgoing[some, :] = dot(rows, source[...].reshape(SLOTS, FF), 0, 0).astype(BF)
            return 0

        lax.fori_loop(0, 8, one, 0)

    in_part(dhg, wg)
    forward_back(2)
    in_part(dhu, wu)

    for k in (0,) + ORDER:
        arrive("r_two", r_two[k])
        arrive("t_two", t_two[k])
    done("own_back", own_back)

    for sent in (one_on, two, two_on):
        leave("gather", sent.values())

    def combine(shard):
        columns = pl.ds(pl.multiple_of(shard * SH, SH), SH)
        return dot(pmat_t[...], back[:, :, :, columns].reshape(SLOTS, SH), 1, 0)

    to_core, to_x = {}, {}

    def for_other_core(k):
        shard = at(k, x) * 2 + 1 - c
        ag[shard] = combine(shard).astype(BF)
        to_core[k] = send(ag.at[shard], xin.at[at(k, x)], xdev(0, 1))

    def for_this_core(k):
        shard = at(k, x) * 2 + c
        part = combine(shard)
        arrive("to_core", [to_core[k]])
        part = part + xin[at(k, x)].astype(F32)
        if k:
            ag[shard] = part.astype(BF)
            to_x[k] = send(ag.at[shard], xin.at[4 + x], xdev(k, 0))
        return part

    for_other_core(2)
    for_other_core(1)
    for_this_core(2)
    for_other_core(3)
    for_this_core(1)
    for_other_core(0)
    for_this_core(3)
    total = for_this_core(0)

    slot_no = lax.broadcasted_iota(jnp.int32, (SLOTS, 128), 0) // CAP
    in_place = slot_no == lax.broadcasted_iota(jnp.int32, (SLOTS, 128), 1)
    spread = jnp.where(in_place, back[:, :, :, D:WIDE].reshape(SLOTS, 128).astype(F32), 0.0)
    values = dot(pmat_t[...], spread.astype(BF), 1, 0).T
    total_gates = jnp.zeros((TOP, TOK), F32)
    for d in range(16):
        wanted = (col + d * 8).astype(F32)
        total_gates += jnp.where(mine == wanted, values[d : d + 1, :], 0.0)
    gsend[...] = total_gates
    grecv_gates[col] = gsend[...]
    gate_sent = []
    for m in (0, 1, 3, 2):
        for f in range(2):
            if (m, f) != (0, 0):
                gate_sent.append(send(gsend, grecv_gates.at[col], xdev(m, f)))

    for k in ORDER:
        arrive("to_x", [to_x[k]])
        total = total + xin[4 + at(-k, x)].astype(F32)
    out_in[...] = total.astype(BF)

    arrive("gate_sent", gate_sent)
    out_gates[...] = jnp.sum(grecv_gates[...], axis=0).astype(BF)

    leave("first", x_own + s_one + s_two)
    leave("gather", one.values())
    leave("g_sent", g_sent.values())
    for k in ORDER:
        leave("rows", p_two[k] + q_two[k])
    for k in (0,) + ORDER:
        leave("back", r_two[k] + t_two[k])
    for k in ORDER:
        leave("back", [r_one[k], t_one[k]])
    leave("sums", gate_sent + list(to_core.values()) + list(to_x.values()))


def write_out(*refs):
    sem = refs[10]
    copies = [pltpu.make_async_copy(refs[n], refs[5 + n], sem.at[n]) for n in range(5)]
    for copy in copies:
        copy.start()
    for copy in copies:
        copy.wait()


def body(inputs, grad_output, gates, expert_ids, owner, w_gate, w_up, w_down):
    vmem, anywhere = pl.BlockSpec(memory_space=pltpu.VMEM), pl.BlockSpec(memory_space=pl.ANY)
    scratch = [
        ((8, TOK, SH), BF),
        ((16, TOK, SH), BF),
        ((16, 8, TOK), F32),
        ((8, 4, 4, CAP, SH), BF),
        ((8, 4, 4, CAP, SH), BF),
        ((4, 4, CAP, WIDE), BF),
        ((4, 4, HALF, WIDE), BF),
        ((4, 4, HALF, WIDE), BF),
        ((4, 4, CAP, WIDE), BF),
        ((4, 4, CAP, FF), F32),
        ((4, 4, CAP, FF), BF),
        ((4, 4, CAP, FF), BF),
        ((4, 4, CAP, FF), BF),
        ((256, FF), BF),
        ((256, FF), BF),
        ((4, 4, HALF, WIDE), BF),
        ((4, 4, HALF, WIDE), BF),
        ((4, 4, CAP, WIDE), BF),
        ((SLOTS, TOK), BF),
        ((TOK, SLOTS), BF),
        ((TOK, TOK), BF),
        ((32, TOK), F32),
        ((TOK, TOK), BF),
        ((8, TOK), F32),
        ((8, 8, TOK), F32),
    ]
    results = [
        ((TOK, SH), BF),
        ((TOP, TOK), BF),
        ((D, FF), BF),
        ((D, FF), BF),
        ((FF, D), BF),
    ]
    held = pl.pallas_call(
        kernel,
        out_shape=[pltpu.VMEM(shape, kind) for shape, kind in results],
        in_specs=[anywhere, anywhere, vmem, vmem, vmem, anywhere, anywhere, anywhere],
        out_specs=[vmem] * 5,
        scratch_shapes=[pltpu.VMEM(shape, kind) for shape, kind in scratch]
        + [
            pltpu.SemaphoreType.DMA((SEMS,)),
            pltpu.SemaphoreType.DMA((SEMS,)),
            pltpu.SemaphoreType.DMA((SEMS // 4,)),
        ],
        compiler_params=pltpu.CompilerParams(
            collective_id=0, has_side_effects=True, vmem_limit_bytes=53 << 20
        ),
    )(
        inputs,
        grad_output,
        expert_ids.T,
        gates.T,
        owner.reshape(1, -1),
        w_gate[0],
        w_up[0],
        w_down[0],
    )
    grad_inputs, grad_gates, grad_gate, grad_up, grad_down = pl.pallas_call(
        write_out,
        out_shape=[jax.ShapeDtypeStruct(shape, kind) for shape, kind in results],
        in_specs=[vmem] * 5,
        out_specs=[anywhere] * 5,
        scratch_shapes=[pltpu.SemaphoreType.DMA((5,))],
        compiler_params=pltpu.CompilerParams(vmem_limit_bytes=16 << 20),
    )(*[pltpu.with_memory_space_constraint(array, pltpu.VMEM) for array in held])
    return (
        grad_inputs,
        grad_gates.T,
        grad_gate[None],
        grad_up[None],
        grad_down[None],
    )


def solution(mesh):
    in_specs = (
        P("dp", "expert"),
        P("dp", "expert"),
        P("dp", None),
        P("dp", None),
        P(),
        P(("dp", "expert"), None, None),
        P(("dp", "expert"), None, None),
        P(("dp", "expert"), None, None),
    )
    out_specs = (
        P("dp", "expert"),
        P("dp", None),
        P(("dp", "expert"), None, None),
        P(("dp", "expert"), None, None),
        P(("dp", "expert"), None, None),
    )
    return jax.shard_map(body, mesh=mesh, in_specs=in_specs, out_specs=out_specs, check_vma=False)
```

```python
import jax
import jax.numpy as jnp
from jax import lax
from jax.experimental import pallas as pl
from jax.experimental.pallas import tpu as pltpu
from jax.sharding import PartitionSpec as P

D, FF, TOP, TOK, CAP = 2048, 768, 8, 512, 64
HALF = CAP // 2
SH = 256
WIDE = D + 128
SLOTS = 1024
SEMS = 208
BF, F32 = jnp.bfloat16, jnp.float32
MESH = pl.DeviceIdType.MESH
ORDER = (1, 3, 2)


def dot(left, right, dim_left, dim_right):
    return lax.dot_general(
        left, right, (((dim_left,), (dim_right,)), ((), ())), preferred_element_type=F32
    )


def iota(shape, dim):
    return lax.broadcasted_iota(jnp.int32, shape, dim).astype(F32)


def kernel(
    inp, gro, ids, gates, owner, wg_in, wu_in, wd_in,
    out_in, out_gates, wg, wu, wd,
    xin, ag, slots, gpack, grecv, pack, st1, st2, fin, dz, act, dhg, dhu, some_g, some_u,
    bst1, bst2, back, pmat, pmat_t, tri, rall, onehot, gsend, grecv_gates,
    send_sem, recv_sem, local_sem,
):
    row, col = lax.axis_index("dp"), lax.axis_index("expert")
    z, y = row // 4, row % 4
    x, c = col // 2, col % 2
    counts = {"remote": 0, "local": 0}

    def at(k, base):
        return (base + k + 4) % 4

    def zdev(k):
        return (at(k, z) * 4 + y, col)

    def ydev(k):
        return (z * 4 + at(k, y), col)

    def xdev(k, flip):
        return (row, at(k, x) * 2 + (c + flip) % 2)

    def send(src, dst, device):
        n = counts["remote"]
        counts["remote"] = n + 1
        copy = pltpu.make_async_remote_copy(
            src_ref=src, dst_ref=dst, send_sem=send_sem.at[n], recv_sem=recv_sem.at[n],
            device_id=device, device_id_type=MESH,
        )
        copy.start()
        return copy

    def local(src, dst):
        n = counts["local"]
        counts["local"] = n + 1
        copy = pltpu.make_async_copy(src, dst, local_sem.at[n])
        copy.start()
        return copy

    def arrive(label, copies):
        for copy in copies:
            copy.wait_recv()

    def leave(label, copies):
        for copy in copies:
            copy.wait_send()

    def done(label, copies):
        for copy in copies:
            copy.wait()

    weights = [local(wg_in, wg), local(wu_in, wu), local(wd_in, wd)]
    own_in, own_gro = local(inp, xin.at[col]), local(gro, ag.at[row])

    barrier = pltpu.get_barrier_semaphore()
    peers = [zdev(k) for k in ORDER] + [ydev(k) for k in ORDER]
    peers += [xdev(k, f) for k in range(4) for f in range(2) if (k, f) != (0, 0)]
    for peer in peers:
        pl.semaphore_signal(barrier, inc=1, device_id=peer, device_id_type=MESH)
    pl.semaphore_wait(barrier, len(peers))

    x_own = [send(inp, xin.at[col], xdev(k, 0)) for k in ORDER]
    x_core = [send(inp, xin.at[col], xdev(0, 1))]
    def half(path):
        return pl.ds(path * 256, 256)

    def quarter(path, n):
        return pl.ds(path * 256 + n * 128, 128)

    def along(path, stage, k):
        return ydev(k) if path == stage - 1 else zdev(k)

    def row_at(path, near, far):
        if path == 0:
            return at(far, z) * 4 + at(near, y)
        return at(near, z) * 4 + at(far, y)

    both = (1, -1)
    one, two, one_on, two_on = {}, {}, {}, {}
    for path in range(2):
        for k in both:
            one[path, k] = send(
                gro.at[half(path)], ag.at[row, half(path)], along(path, 1, k)
            )
    for path in range(2):
        for k in both:
            two[path, 0, k] = send(
                gro.at[half(path)], ag.at[row, half(path)], along(path, 2, k)
            )

    def pass_block(path, near):
        here = ag.at[row_at(path, near, 0), half(path)]
        for k in both:
            two[path, near, k] = send(here, here, along(path, 2, k))

    def pass_on(path, stage, near, k):
        source = row_at(path, -k, 0) if stage == 1 else row_at(path, near, -k)
        here = ag.at[source, quarter(path, 0 if k == 1 else 1)]
        return send(here, here, along(path, stage, k))

    tri[...] = (iota((TOK, TOK), 0) <= iota((TOK, TOK), 1)).astype(BF)
    expert_no = lax.broadcasted_iota(jnp.int32, (128, TOK), 0)
    owner_row = jnp.broadcast_to(owner[...].astype(F32), (8, 128)).astype(BF)
    for k in range(TOP):
        match = (ids[k : k + 1, :] == expert_no).astype(F32).astype(BF)
        slots[row, k : k + 1, :] = dot(owner_row, match, 1, 0)[0:1, :]
    s_one = [send(slots.at[row], slots.at[row], ydev(k)) for k in ORDER]

    mine = slots[row]
    name = iota((16, TOK), 0) * 8.0 + col.astype(F32)
    member = jnp.zeros((16, TOK), F32)
    gate_of = jnp.zeros((16, TOK), F32)
    for k in range(TOP):
        hit = mine[k : k + 1, :] == name
        member += jnp.where(hit, 1.0, 0.0)
        gate_of += jnp.where(hit, gates[k : k + 1, :].astype(F32), 0.0)
    rank = dot(member.astype(BF), tri[...], 1, 0) * member
    place = iota((CAP, TOK), 0) + 1.0
    for d in range(16):
        hot = jnp.where(rank[d : d + 1, :] == place, 1.0, 0.0)
        pmat[d * CAP : (d + 1) * CAP, :] = hot.astype(BF)
        gate_col = jnp.sum(hot * gate_of[d : d + 1, :], axis=1, keepdims=True)
        pack[d // 4, d % 4, :, D:WIDE] = jnp.broadcast_to(gate_col, (CAP, 128)).astype(BF)

    arrive("slots", s_one)
    s_two = [
        send(slots.at[pl.ds(z * 4, 4)], slots.at[pl.ds(z * 4, 4)], zdev(k)) for k in ORDER
    ]

    neighbours = iota((8, TOK), 0) + row.astype(F32) * 8.0

    def rank_members(group):
        def one(step, _):
            found = jnp.zeros((8, TOK), F32)
            theirs = slots[group * 4 + step]
            for k in range(TOP):
                found += jnp.where(theirs[k : k + 1, :] == neighbours, 1.0, 0.0)
            rall[pl.ds(pl.multiple_of(step * 8, 8), 8), :] = found
            return 0

        lax.fori_loop(0, 4, one, 0)
        rall[...] = dot(rall[...].astype(BF), tri[...], 1, 0) * rall[...]

    def pack_gradients(group):
        rank_members(group)

        def one(step, _):
            r = group * 4 + step
            ranks = rall[pl.ds(pl.multiple_of(step * 8, 8), 8), :]
            for e in range(8):
                hot = jnp.where(ranks[e : e + 1, :] == place, 1.0, 0.0)
                onehot[e * CAP : (e + 1) * CAP, :] = hot.astype(BF)
            rows = dot(onehot[...], ag[r], 1, 0).astype(BF)
            gpack[:, group, step] = rows.reshape(8, CAP, SH)
            return 0

        lax.fori_loop(0, 4, one, 0)

    g_sent = {}
    own_grads = []

    def exchange_gradients(group, k):
        for m in (0, 1, 3, 2):
            for f in range(2):
                target = at(m, x) * 2 + (c + f) % 2
                if (m, f) == (0, 0):
                    own_grads.append(local(gpack.at[col, group], grecv.at[col, group]))
                else:
                    g_sent[k, m, f] = send(
                        gpack.at[target, group], grecv.at[col, group], xdev(m, f)
                    )

    for path in range(2):
        for k in both:
            arrive("one", [one[path, k]])
            one_on[path, k] = pass_on(path, 1, 0, k)
            pass_block(path, -k)
    for path in range(2):
        for k in both:
            arrive("two", [two[path, 0, k]])
            two_on[path, 0, k] = pass_on(path, 2, 0, k)
    for path in range(2):
        arrive("one_on", [one_on[path, k] for k in both])
        pass_block(path, 2)
    for n, k in enumerate(ORDER):
        arrive("x_own", [x_own[n]])
        source = at(-k, x) * 2 + c
        x_core.append(send(xin.at[source], xin.at[source], xdev(0, 1)))

    def pass_far(near):
        for path in range(2):
            for k in both:
                arrive("two", [two[path, near, k]])
                two_on[path, near, k] = pass_on(path, 2, near, k)

    arrive("two_on", [two_on[1, 0, k] for k in both])
    own_gro.wait()
    pack_gradients(z)
    exchange_gradients(z, 0)

    pass_far(-1)

    arrive("x_core", x_core)
    own_in.wait()

    def pack_inputs(shard, _):
        rows = dot(pmat[...], xin[shard], 1, 0).astype(BF)
        pack[:, :, :, pl.ds(pl.multiple_of(shard * SH, SH), SH)] = rows.reshape(4, 4, CAP, SH)
        return 0

    lax.fori_loop(0, 8, pack_inputs, 0)

    first, second = pl.ds(0, HALF), pl.ds(HALF, HALF)
    p_two = {0: [send(pack.at[at(k, z), y, first], fin.at[z, y, first], zdev(k)) for k in ORDER]}
    q_two = {0: [send(pack.at[z, at(k, y), second], fin.at[z, y, second], ydev(k)) for k in ORDER]}
    own_rows = [local(pack.at[z, y], fin.at[z, y])]

    pass_far(1)
    pass_far(2)
    p_one = [send(pack.at[:, at(k, y), first], st1.at[y], ydev(k)) for k in ORDER]
    q_one = [send(pack.at[at(k, z), :, second], st2.at[z], zdev(k)) for k in ORDER]

    leave("x_core", x_core)
    arrive("slots_two", s_two)
    for k, near in zip(ORDER, (-1, 1, 2)):
        arrive("two_on", [two_on[1, near, m] for m in both])
        if k == 2:
            arrive("two_on", [two_on[0, n, m] for n in (0, -1, 1, 2) for m in both])
        group = at(-k, z)
        pack_gradients(group)
        exchange_gradients(group, k)

    for n, k in enumerate(ORDER):
        arrive("p_one", [p_one[n]])
        source = at(-k, y)
        p_two[k] = [
            send(st1.at[source, at(m, z)], fin.at[z, source, first], zdev(m)) for m in ORDER
        ]
        own_rows.append(local(st1.at[source, z], fin.at[z, source, first]))
        arrive("q_one", [q_one[n]])
        source = at(-k, z)
        q_two[k] = [
            send(st2.at[source, at(m, y)], fin.at[source, y, second], ydev(m)) for m in ORDER
        ]
        own_rows.append(local(st2.at[source, y], fin.at[source, y, second]))

    pmat_t[...] = pmat[...].T

    done("weights", weights + own_grads)

    def add_dz(shard, start):
        columns = pl.ds(pl.multiple_of(shard * SH, SH), SH)

        def chunk(n, _):
            part = dot(grecv[shard, n].reshape(256, SH), wd[:, columns], 1, 1)
            part = part.reshape(4, CAP, FF)
            dz[n] = part if start else dz[n] + part
            return 0

        lax.fori_loop(0, 4, chunk, 0)

    add_dz(col, True)
    for m in (0, 1, 3, 2):
        for f in range(2):
            if (m, f) != (0, 0):
                arrive("grads", [g_sent[k, m, f] for k in (0, 1, 3, 2)])
                add_dz(at(-m, x) * 2 + (c + f) % 2, False)

    leave("pack", p_one + q_one + p_two[0] + q_two[0])
    done("own_rows", own_rows)

    def chunk_of(ref, zk, yk, width):
        lower_rows = ref[zk, :, 0:HALF, 0:width].reshape(4 * HALF, width)
        upper_rows = ref[:, yk, HALF:CAP, 0:width].reshape(4 * HALF, width)
        return jnp.concatenate([lower_rows, upper_rows], axis=0)

    def put_chunk(ref, zk, yk, columns, value):
        width = value.shape[1]
        ref[zk, :, 0:HALF, columns] = value[: 4 * HALF].reshape(4, HALF, width)
        ref[:, yk, HALF:CAP, columns] = value[4 * HALF :].reshape(4, HALF, width)

    def through_expert(zk, yk):
        rows = chunk_of(fin, zk, yk, WIDE)
        gate_col = rows[:, D : D + 1].astype(F32)
        h1 = dot(rows[:, :D], wg[...], 1, 0)
        h2 = dot(rows[:, :D], wu[...], 1, 0)
        dz_here = chunk_of(dz, zk, yk, FF)
        sigma = jax.nn.sigmoid(h1)
        silu = h1 * sigma
        slope = sigma * (1.0 + h1 * (1.0 - sigma))
        acted = (silu * h2).astype(BF)
        every = pl.ds(0, FF)
        put_chunk(act, zk, yk, every, acted)
        gate_grad = jnp.sum(acted.astype(F32) * dz_here, axis=1, keepdims=True)
        put_chunk(pack, zk, yk, pl.ds(D, 128), jnp.broadcast_to(gate_grad, (256, 128)).astype(BF))
        dfa = gate_col * dz_here
        some_g[...] = (dfa * h2 * slope).astype(BF)
        some_u[...] = (dfa * silu).astype(BF)
        put_chunk(dhg, zk, yk, every, some_g[...])
        put_chunk(dhu, zk, yk, every, some_u[...])

        def back_part(n, _):
            some = pl.ds(pl.multiple_of(n * 512, 512), 512)
            part = dot(some_g[...], wg[some, :], 1, 1) + dot(some_u[...], wu[some, :], 1, 1)
            part = part.astype(BF)
            for h in range(2):
                pieces = [part[:, m * 128 : m * 128 + 128] for m in (h, h + 2)]
                columns = pl.ds(pl.multiple_of(h * 1024 + n * 256, 256), 256)
                put_chunk(pack, zk, yk, columns, jnp.concatenate(pieces, axis=1))
            return 0

        lax.fori_loop(0, 4, back_part, 0)

    r_one, t_one, r_two, t_two, own_back = {}, {}, {}, {}, ([], [])
    lanes = (pl.ds(0, D // 2), pl.ds(D // 2, WIDE - D // 2))

    def forward_back(k, h):
        part = lanes[h]
        arrive("r_one", [r_one[k, h]])
        source = at(k, z)
        r_two[k, h] = [
            send(
                bst1.at[source, at(m, y), :, part], back.at[source, y, first, part], ydev(m)
            )
            for m in ORDER
        ]
        own_back[h].append(local(bst1.at[source, y, :, part], back.at[source, y, first, part]))
        arrive("t_one", [t_one[k, h]])
        source = at(k, y)
        t_two[k, h] = [
            send(
                bst2.at[source, at(m, z), :, part], back.at[z, source, second, part], zdev(m)
            )
            for m in ORDER
        ]
        own_back[h].append(local(bst2.at[source, z, :, part], back.at[z, source, second, part]))

    for k in (0,) + ORDER:
        zk, yk = at(-k, z), at(-k, y)
        if k:
            n = ORDER.index(k)
            arrive("rows", [p_two[source][n] for source in (0, 1, 3, 2)])
            arrive("rows", [q_two[source][n] for source in (0, 1, 3, 2)])
        through_expert(zk, yk)
        for h, part in enumerate(lanes):
            if k:
                r_one[k, h] = send(
                    pack.at[zk, :, first, part], bst1.at[z, :, :, part], zdev(-k)
                )
                t_one[k, h] = send(
                    pack.at[:, yk, second, part], bst2.at[y, :, :, part], ydev(-k)
                )
            else:
                r_two[0, h] = [
                    send(
                        pack.at[z, at(m, y), first, part], back.at[z, y, first, part], ydev(m)
                    )
                    for m in ORDER
                ]
                t_two[0, h] = [
                    send(
                        pack.at[at(m, z), y, second, part], back.at[z, y, second, part], zdev(m)
                    )
                    for m in ORDER
                ]
                own_back[h].append(local(pack.at[z, y, :, part], back.at[z, y, :, part]))

    gate_all = fin[:, :, :, D : D + 1].reshape(SLOTS, 1).astype(F32)

    def down_part(shard, _):
        grads = grecv[shard].reshape(SLOTS, SH).astype(F32)
        scaled = (gate_all * grads).astype(BF)
        columns = pl.ds(pl.multiple_of(shard * SH, SH), SH)
        wd[:, columns] = dot(act[...].reshape(SLOTS, FF), scaled, 0, 0).astype(BF)
        return 0

    lax.fori_loop(0, 4, down_part, 0)
    forward_back(1, 0)
    forward_back(1, 1)
    lax.fori_loop(4, 8, down_part, 0)
    forward_back(3, 0)

    def in_part(source, outgoing):
        def one(n, _):
            some = pl.ds(pl.multiple_of(n * 256, 256), 256)
            rows = fin[:, :, :, some].reshape(SLOTS, 256)
            outgoing[some, :] = dot(rows, source[...].reshape(SLOTS, FF), 0, 0).astype(BF)
            return 0

        lax.fori_loop(0, 8, one, 0)

    in_part(dhg, wg)
    forward_back(2, 0)
    forward_back(3, 1)
    forward_back(2, 1)
    in_part(dhu, wu)

    leave("gather", list(one_on.values()) + list(two.values()) + list(two_on.values()))
    to_core, to_x, own_sum = {}, {}, {}
    sums_at = (pl.ds(0, 128), pl.ds(128, 128))

    def sum_pair(k, h):
        columns = pl.ds(pl.multiple_of(h * 1024 + at(k, x) * 256, 256), 256)
        pair = dot(pmat_t[...], back[:, :, :, columns].reshape(SLOTS, 256), 1, 0)
        ours = jnp.where(c == 0, pair[:, :128], pair[:, 128:])
        theirs = jnp.where(c == 0, pair[:, 128:], pair[:, :128])
        for n in range(2):
            dz[k, :, :, n * 128 : n * 128 + 128] = ours[n * 256 : n * 256 + 256].reshape(4, CAP, 128)
        ag[k, :, sums_at[h]] = theirs.astype(BF)
        to_core[k, h] = send(ag.at[k, :, sums_at[h]], xin.at[at(k, x), :, sums_at[h]], xdev(0, 1))

    def send_sum(k, h):
        arrive("to_core", [to_core[k, h]])
        ours = [dz[k, :, :, n * 128 : n * 128 + 128].reshape(256, 128) for n in range(2)]
        part = jnp.concatenate(ours, axis=0) + xin[at(k, x), :, sums_at[h]].astype(F32)
        if k:
            ag[4 + k, :, sums_at[h]] = part.astype(BF)
            to_x[k, h] = send(ag.at[4 + k, :, sums_at[h]], xin.at[4 + x, :, sums_at[h]], xdev(k, 0))
        else:
            own_sum[h] = part

    for h in range(2):
        for k in (0,) + ORDER:
            arrive("r_two", r_two[k, h])
            arrive("t_two", t_two[k, h])
        done("own_back", own_back[h])
        sum_pair(2, h)
        sum_pair(1, h)
        send_sum(2, h)
        sum_pair(3, h)
        send_sum(1, h)
        sum_pair(0, h)
        send_sum(3, h)
        send_sum(0, h)

    slot_no = lax.broadcasted_iota(jnp.int32, (SLOTS, 128), 0) // CAP
    in_place = slot_no == lax.broadcasted_iota(jnp.int32, (SLOTS, 128), 1)
    spread = jnp.where(in_place, back[:, :, :, D:WIDE].reshape(SLOTS, 128).astype(F32), 0.0)
    values = dot(pmat_t[...], spread.astype(BF), 1, 0).T
    total_gates = jnp.zeros((TOP, TOK), F32)
    for d in range(16):
        wanted = (col + d * 8).astype(F32)
        total_gates += jnp.where(mine == wanted, values[d : d + 1, :], 0.0)
    gsend[...] = total_gates
    grecv_gates[col] = gsend[...]
    gate_sent = []
    for m in (0, 1, 3, 2):
        for f in range(2):
            if (m, f) != (0, 0):
                gate_sent.append(send(gsend, grecv_gates.at[col], xdev(m, f)))

    for h in range(2):
        total = own_sum[h]
        for k in ORDER:
            arrive("to_x", [to_x[k, h]])
            total = total + xin[4 + at(-k, x), :, sums_at[h]].astype(F32)
        out_in[:, sums_at[h]] = total.astype(BF)

    arrive("gate_sent", gate_sent)
    out_gates[...] = jnp.sum(grecv_gates[...], axis=0).astype(BF)

    leave("first", x_own + s_one + s_two)
    leave("gather", one.values())
    leave("g_sent", g_sent.values())
    for k in ORDER:
        leave("rows", p_two[k] + q_two[k])
    for h in range(2):
        for k in (0,) + ORDER:
            leave("back", r_two[k, h] + t_two[k, h])
        for k in ORDER:
            leave("back", [r_one[k, h], t_one[k, h]])
    leave("sums", gate_sent + list(to_core.values()) + list(to_x.values()))


def write_out(*refs):
    sem = refs[10]
    copies = [pltpu.make_async_copy(refs[n], refs[5 + n], sem.at[n]) for n in range(5)]
    for copy in copies:
        copy.start()
    for copy in copies:
        copy.wait()


def body(inputs, grad_output, gates, expert_ids, owner, w_gate, w_up, w_down):
    vmem, anywhere = pl.BlockSpec(memory_space=pltpu.VMEM), pl.BlockSpec(memory_space=pl.ANY)
    scratch = [
        ((8, TOK, SH), BF),
        ((16, TOK, SH), BF),
        ((16, 8, TOK), F32),
        ((8, 4, 4, CAP, SH), BF),
        ((8, 4, 4, CAP, SH), BF),
        ((4, 4, CAP, WIDE), BF),
        ((4, 4, HALF, WIDE), BF),
        ((4, 4, HALF, WIDE), BF),
        ((4, 4, CAP, WIDE), BF),
        ((4, 4, CAP, FF), F32),
        ((4, 4, CAP, FF), BF),
        ((4, 4, CAP, FF), BF),
        ((4, 4, CAP, FF), BF),
        ((256, FF), BF),
        ((256, FF), BF),
        ((4, 4, HALF, WIDE), BF),
        ((4, 4, HALF, WIDE), BF),
        ((4, 4, CAP, WIDE), BF),
        ((SLOTS, TOK), BF),
        ((TOK, SLOTS), BF),
        ((TOK, TOK), BF),
        ((32, TOK), F32),
        ((TOK, TOK), BF),
        ((8, TOK), F32),
        ((8, 8, TOK), F32),
    ]
    results = [
        ((TOK, SH), BF),
        ((TOP, TOK), BF),
        ((D, FF), BF),
        ((D, FF), BF),
        ((FF, D), BF),
    ]
    held = pl.pallas_call(
        kernel,
        out_shape=[pltpu.VMEM(shape, kind) for shape, kind in results],
        in_specs=[anywhere, anywhere, vmem, vmem, vmem, anywhere, anywhere, anywhere],
        out_specs=[vmem] * 5,
        scratch_shapes=[pltpu.VMEM(shape, kind) for shape, kind in scratch]
        + [
            pltpu.SemaphoreType.DMA((SEMS,)),
            pltpu.SemaphoreType.DMA((SEMS,)),
            pltpu.SemaphoreType.DMA((SEMS // 4,)),
        ],
        compiler_params=pltpu.CompilerParams(
            collective_id=0, has_side_effects=True, vmem_limit_bytes=53 << 20
        ),
    )(
        inputs,
        grad_output,
        expert_ids.T,
        gates.T,
        owner.reshape(1, -1),
        w_gate[0],
        w_up[0],
        w_down[0],
    )
    grad_inputs, grad_gates, grad_gate, grad_up, grad_down = pl.pallas_call(
        write_out,
        out_shape=[jax.ShapeDtypeStruct(shape, kind) for shape, kind in results],
        in_specs=[vmem] * 5,
        out_specs=[anywhere] * 5,
        scratch_shapes=[pltpu.SemaphoreType.DMA((5,))],
        compiler_params=pltpu.CompilerParams(vmem_limit_bytes=16 << 20),
    )(*[pltpu.with_memory_space_constraint(array, pltpu.VMEM) for array in held])
    return (
        grad_inputs,
        grad_gates.T,
        grad_gate[None],
        grad_up[None],
        grad_down[None],
    )


def solution(mesh):
    in_specs = (
        P("dp", "expert"),
        P("dp", "expert"),
        P("dp", None),
        P("dp", None),
        P(),
        P(("dp", "expert"), None, None),
        P(("dp", "expert"), None, None),
        P(("dp", "expert"), None, None),
    )
    out_specs = (
        P("dp", "expert"),
        P("dp", None),
        P(("dp", "expert"), None, None),
        P(("dp", "expert"), None, None),
        P(("dp", "expert"), None, None),
    )
    return jax.shard_map(body, mesh=mesh, in_specs=in_specs, out_specs=out_specs, check_vma=False)
```

```python
import jax
import jax.numpy as jnp
from jax import lax
from jax.experimental import pallas as pl
from jax.experimental.pallas import tpu as pltpu
from jax.sharding import PartitionSpec as P

D, FF, TOP, TOK, CAP = 2048, 768, 8, 512, 64
HALF = CAP // 2
SH = 256
WIDE = D + 128
SLOTS = 1024
SEMS = 208
BF, F32 = jnp.bfloat16, jnp.float32
MESH = pl.DeviceIdType.MESH
ORDER = (1, 3, 2)


def dot(left, right, dim_left, dim_right):
    return lax.dot_general(
        left, right, (((dim_left,), (dim_right,)), ((), ())), preferred_element_type=F32
    )


def iota(shape, dim):
    return lax.broadcasted_iota(jnp.int32, shape, dim).astype(F32)


def kernel(
    inp, gro, ids, gates, owner, wg_in, wu_in, wd_in,
    out_in, out_gates, wg, wu, wd,
    xin, ag, slots, gpack, grecv, pack, st1, st2, fin, dz, act, dhg, dhu, some_g, some_u,
    bst1, bst2, back, pmat, pmat_t, tri, rall, onehot, gsend, grecv_gates,
    send_sem, recv_sem, local_sem,
):
    row, col = lax.axis_index("dp"), lax.axis_index("expert")
    z, y = row // 4, row % 4
    x, c = col // 2, col % 2
    counts = {"remote": 0, "local": 0}

    def at(k, base):
        return (base + k + 4) % 4

    def zdev(k):
        return (at(k, z) * 4 + y, col)

    def ydev(k):
        return (z * 4 + at(k, y), col)

    def xdev(k, flip):
        return (row, at(k, x) * 2 + (c + flip) % 2)

    def send(src, dst, device):
        n = counts["remote"]
        counts["remote"] = n + 1
        copy = pltpu.make_async_remote_copy(
            src_ref=src, dst_ref=dst, send_sem=send_sem.at[n], recv_sem=recv_sem.at[n],
            device_id=device, device_id_type=MESH,
        )
        copy.start()
        return copy

    def local(src, dst):
        n = counts["local"]
        counts["local"] = n + 1
        copy = pltpu.make_async_copy(src, dst, local_sem.at[n])
        copy.start()
        return copy

    def arrive(label, copies):
        for copy in copies:
            copy.wait_recv()

    def leave(label, copies):
        for copy in copies:
            copy.wait_send()

    def done(label, copies):
        for copy in copies:
            copy.wait()

    weights = [local(wg_in, wg), local(wu_in, wu), local(wd_in, wd)]
    own_in, own_gro = local(inp, xin.at[col]), local(gro, ag.at[row])

    barrier = pltpu.get_barrier_semaphore()
    peers = [zdev(k) for k in ORDER] + [ydev(k) for k in ORDER]
    peers += [xdev(k, f) for k in range(4) for f in range(2) if (k, f) != (0, 0)]
    for peer in peers:
        pl.semaphore_signal(barrier, inc=1, device_id=peer, device_id_type=MESH)
    pl.semaphore_wait(barrier, len(peers))

    x_own = [send(inp, xin.at[col], xdev(k, 0)) for k in ORDER]
    x_core = [send(inp, xin.at[col], xdev(0, 1))]
    def half(path):
        return pl.ds(path * 256, 256)

    def quarter(path, n):
        return pl.ds(path * 256 + n * 128, 128)

    def along(path, stage, k):
        return ydev(k) if path == stage - 1 else zdev(k)

    def row_at(path, near, far):
        if path == 0:
            return at(far, z) * 4 + at(near, y)
        return at(near, z) * 4 + at(far, y)

    both = (1, -1)
    one, two, one_on, two_on = {}, {}, {}, {}
    for path in range(2):
        for k in both:
            one[path, k] = send(
                gro.at[half(path)], ag.at[row, half(path)], along(path, 1, k)
            )
    for path in range(2):
        for k in both:
            two[path, 0, k] = send(
                gro.at[half(path)], ag.at[row, half(path)], along(path, 2, k)
            )

    def pass_block(path, near):
        here = ag.at[row_at(path, near, 0), half(path)]
        for k in both:
            two[path, near, k] = send(here, here, along(path, 2, k))

    def pass_on(path, stage, near, k):
        source = row_at(path, -k, 0) if stage == 1 else row_at(path, near, -k)
        here = ag.at[source, quarter(path, 0 if k == 1 else 1)]
        return send(here, here, along(path, stage, k))

    tri[...] = (iota((TOK, TOK), 0) <= iota((TOK, TOK), 1)).astype(BF)
    expert_no = lax.broadcasted_iota(jnp.int32, (128, TOK), 0)
    owner_row = jnp.broadcast_to(owner[...].astype(F32), (8, 128)).astype(BF)
    for k in range(TOP):
        match = (ids[k : k + 1, :] == expert_no).astype(F32).astype(BF)
        slots[row, k : k + 1, :] = dot(owner_row, match, 1, 0)[0:1, :]
    s_one = [send(slots.at[row], slots.at[row], ydev(k)) for k in ORDER]

    mine = slots[row]
    name = iota((16, TOK), 0) * 8.0 + col.astype(F32)
    member = jnp.zeros((16, TOK), F32)
    gate_of = jnp.zeros((16, TOK), F32)
    for k in range(TOP):
        hit = mine[k : k + 1, :] == name
        member += jnp.where(hit, 1.0, 0.0)
        gate_of += jnp.where(hit, gates[k : k + 1, :].astype(F32), 0.0)
    rank = dot(member.astype(BF), tri[...], 1, 0) * member
    place = iota((CAP, TOK), 0) + 1.0
    for d in range(16):
        hot = jnp.where(rank[d : d + 1, :] == place, 1.0, 0.0)
        pmat[d * CAP : (d + 1) * CAP, :] = hot.astype(BF)
        gate_col = jnp.sum(hot * gate_of[d : d + 1, :], axis=1, keepdims=True)
        pack[d // 4, d % 4, :, D:WIDE] = jnp.broadcast_to(gate_col, (CAP, 128)).astype(BF)

    arrive("slots", s_one)
    s_two = [
        send(slots.at[pl.ds(z * 4, 4)], slots.at[pl.ds(z * 4, 4)], zdev(k)) for k in ORDER
    ]

    neighbours = iota((8, TOK), 0) + row.astype(F32) * 8.0

    def rank_members(group):
        def one(step, _):
            found = jnp.zeros((8, TOK), F32)
            theirs = slots[group * 4 + step]
            for k in range(TOP):
                found += jnp.where(theirs[k : k + 1, :] == neighbours, 1.0, 0.0)
            rall[pl.ds(pl.multiple_of(step * 8, 8), 8), :] = found
            return 0

        lax.fori_loop(0, 4, one, 0)
        rall[...] = dot(rall[...].astype(BF), tri[...], 1, 0) * rall[...]

    def pack_gradients(group):
        rank_members(group)

        def one(step, _):
            r = group * 4 + step
            ranks = rall[pl.ds(pl.multiple_of(step * 8, 8), 8), :]
            for e in range(8):
                hot = jnp.where(ranks[e : e + 1, :] == place, 1.0, 0.0)
                onehot[e * CAP : (e + 1) * CAP, :] = hot.astype(BF)
            rows = dot(onehot[...], ag[r], 1, 0).astype(BF)
            gpack[:, group, step] = rows.reshape(8, CAP, SH)
            return 0

        lax.fori_loop(0, 4, one, 0)

    g_sent = {}
    own_grads = []

    def exchange_gradients(group, k):
        for m in (0, 1, 3, 2):
            for f in range(2):
                target = at(m, x) * 2 + (c + f) % 2
                if (m, f) == (0, 0):
                    own_grads.append(local(gpack.at[col, group], grecv.at[col, group]))
                else:
                    g_sent[k, m, f] = send(
                        gpack.at[target, group], grecv.at[col, group], xdev(m, f)
                    )

    for path in range(2):
        for k in both:
            arrive("one", [one[path, k]])
            one_on[path, k] = pass_on(path, 1, 0, k)
            pass_block(path, -k)
    for path in range(2):
        for k in both:
            arrive("two", [two[path, 0, k]])
            two_on[path, 0, k] = pass_on(path, 2, 0, k)
    for path in range(2):
        arrive("one_on", [one_on[path, k] for k in both])
        pass_block(path, 2)
    for n, k in enumerate(ORDER):
        arrive("x_own", [x_own[n]])
        source = at(-k, x) * 2 + c
        x_core.append(send(xin.at[source], xin.at[source], xdev(0, 1)))

    def pass_far(near):
        for path in range(2):
            for k in both:
                arrive("two", [two[path, near, k]])
                two_on[path, near, k] = pass_on(path, 2, near, k)

    arrive("two_on", [two_on[1, 0, k] for k in both])
    own_gro.wait()
    pack_gradients(z)
    exchange_gradients(z, 0)

    pass_far(-1)

    arrive("x_core", x_core)
    own_in.wait()

    def pack_inputs(shard, _):
        rows = dot(pmat[...], xin[shard], 1, 0).astype(BF)
        pack[:, :, :, pl.ds(pl.multiple_of(shard * SH, SH), SH)] = rows.reshape(4, 4, CAP, SH)
        return 0

    lax.fori_loop(0, 8, pack_inputs, 0)

    first, second = pl.ds(0, HALF), pl.ds(HALF, HALF)
    p_two = {0: [send(pack.at[at(k, z), y, first], fin.at[z, y, first], zdev(k)) for k in ORDER]}
    q_two = {0: [send(pack.at[z, at(k, y), second], fin.at[z, y, second], ydev(k)) for k in ORDER]}
    own_rows = [local(pack.at[z, y], fin.at[z, y])]

    pass_far(1)
    pass_far(2)
    p_one = [send(pack.at[:, at(k, y), first], st1.at[y], ydev(k)) for k in ORDER]
    q_one = [send(pack.at[at(k, z), :, second], st2.at[z], zdev(k)) for k in ORDER]

    leave("x_core", x_core)
    arrive("slots_two", s_two)
    for k, near in zip(ORDER, (-1, 1, 2)):
        arrive("two_on", [two_on[1, near, m] for m in both])
        if k == 2:
            arrive("two_on", [two_on[0, n, m] for n in (0, -1, 1, 2) for m in both])
        group = at(-k, z)
        pack_gradients(group)
        exchange_gradients(group, k)

    for n, k in enumerate(ORDER):
        arrive("p_one", [p_one[n]])
        source = at(-k, y)
        p_two[k] = [
            send(st1.at[source, at(m, z)], fin.at[z, source, first], zdev(m)) for m in ORDER
        ]
        own_rows.append(local(st1.at[source, z], fin.at[z, source, first]))
        arrive("q_one", [q_one[n]])
        source = at(-k, z)
        q_two[k] = [
            send(st2.at[source, at(m, y)], fin.at[source, y, second], ydev(m)) for m in ORDER
        ]
        own_rows.append(local(st2.at[source, y], fin.at[source, y, second]))

    pmat_t[...] = pmat[...].T

    done("weights", weights + own_grads)

    def add_dz(shard, start):
        columns = pl.ds(pl.multiple_of(shard * SH, SH), SH)

        def chunk(n, _):
            part = dot(grecv[shard, n].reshape(256, SH), wd[:, columns], 1, 1)
            part = part.reshape(4, CAP, FF)
            dz[n] = part if start else dz[n] + part
            return 0

        lax.fori_loop(0, 4, chunk, 0)

    add_dz(col, True)
    for m in (0, 1, 3, 2):
        for f in range(2):
            if (m, f) != (0, 0):
                arrive("grads", [g_sent[k, m, f] for k in (0, 1, 3, 2)])
                add_dz(at(-m, x) * 2 + (c + f) % 2, False)

    leave("pack", p_one + q_one + p_two[0] + q_two[0])
    done("own_rows", own_rows)

    def chunk_of(ref, zk, yk, width):
        lower_rows = ref[zk, :, 0:HALF, 0:width].reshape(4 * HALF, width)
        upper_rows = ref[:, yk, HALF:CAP, 0:width].reshape(4 * HALF, width)
        return jnp.concatenate([lower_rows, upper_rows], axis=0)

    def put_chunk(ref, zk, yk, columns, value):
        width = value.shape[1]
        ref[zk, :, 0:HALF, columns] = value[: 4 * HALF].reshape(4, HALF, width)
        ref[:, yk, HALF:CAP, columns] = value[4 * HALF :].reshape(4, HALF, width)

    def through_expert(zk, yk):
        rows = chunk_of(fin, zk, yk, WIDE)
        gate_col = rows[:, D : D + 1].astype(F32)
        h1 = dot(rows[:, :D], wg[...], 1, 0)
        h2 = dot(rows[:, :D], wu[...], 1, 0)
        dz_here = chunk_of(dz, zk, yk, FF)
        sigma = jax.nn.sigmoid(h1)
        silu = h1 * sigma
        slope = sigma * (1.0 + h1 * (1.0 - sigma))
        acted = (silu * h2).astype(BF)
        every = pl.ds(0, FF)
        put_chunk(act, zk, yk, every, acted)
        gate_grad = jnp.sum(acted.astype(F32) * dz_here, axis=1, keepdims=True)
        put_chunk(pack, zk, yk, pl.ds(D, 128), jnp.broadcast_to(gate_grad, (256, 128)).astype(BF))
        dfa = gate_col * dz_here
        some_g[...] = (dfa * h2 * slope).astype(BF)
        some_u[...] = (dfa * silu).astype(BF)
        put_chunk(dhg, zk, yk, every, some_g[...])
        put_chunk(dhu, zk, yk, every, some_u[...])

        def back_part(n, _):
            some = pl.ds(pl.multiple_of(n * 512, 512), 512)
            part = dot(some_g[...], wg[some, :], 1, 1) + dot(some_u[...], wu[some, :], 1, 1)
            part = part.astype(BF)
            for h in range(2):
                pieces = [part[:, m * 128 : m * 128 + 128] for m in (h, h + 2)]
                columns = pl.ds(pl.multiple_of(h * 1024 + n * 256, 256), 256)
                put_chunk(pack, zk, yk, columns, jnp.concatenate(pieces, axis=1))
            return 0

        lax.fori_loop(0, 4, back_part, 0)

    r_one, t_one, r_two, t_two, own_back = {}, {}, {}, {}, ([], [])
    lanes = (pl.ds(0, D // 2), pl.ds(D // 2, WIDE - D // 2))

    def forward_back(k, h):
        part = lanes[h]
        arrive("r_one", [r_one[k, h]])
        source = at(k, z)
        r_two[k, h] = [
            send(
                bst1.at[source, at(m, y), :, part], back.at[source, y, first, part], ydev(m)
            )
            for m in ORDER
        ]
        own_back[h].append(local(bst1.at[source, y, :, part], back.at[source, y, first, part]))
        arrive("t_one", [t_one[k, h]])
        source = at(k, y)
        t_two[k, h] = [
            send(
                bst2.at[source, at(m, z), :, part], back.at[z, source, second, part], zdev(m)
            )
            for m in ORDER
        ]
        own_back[h].append(local(bst2.at[source, z, :, part], back.at[z, source, second, part]))

    for k in (0,) + ORDER:
        zk, yk = at(-k, z), at(-k, y)
        if k:
            n = ORDER.index(k)
            arrive("rows", [p_two[source][n] for source in (0, 1, 3, 2)])
            arrive("rows", [q_two[source][n] for source in (0, 1, 3, 2)])
        through_expert(zk, yk)
        for h, part in enumerate(lanes):
            if k:
                r_one[k, h] = send(
                    pack.at[zk, :, first, part], bst1.at[z, :, :, part], zdev(-k)
                )
                t_one[k, h] = send(
                    pack.at[:, yk, second, part], bst2.at[y, :, :, part], ydev(-k)
                )
            else:
                r_two[0, h] = [
                    send(
                        pack.at[z, at(m, y), first, part], back.at[z, y, first, part], ydev(m)
                    )
                    for m in ORDER
                ]
                t_two[0, h] = [
                    send(
                        pack.at[at(m, z), y, second, part], back.at[z, y, second, part], zdev(m)
                    )
                    for m in ORDER
                ]
                own_back[h].append(local(pack.at[z, y, :, part], back.at[z, y, :, part]))

    gate_all = fin[:, :, :, D : D + 1].reshape(SLOTS, 1).astype(F32)

    def down_part(shard, _):
        grads = grecv[shard].reshape(SLOTS, SH).astype(F32)
        scaled = (gate_all * grads).astype(BF)
        columns = pl.ds(pl.multiple_of(shard * SH, SH), SH)
        wd[:, columns] = dot(act[...].reshape(SLOTS, FF), scaled, 0, 0).astype(BF)
        return 0

    lax.fori_loop(0, 4, down_part, 0)
    forward_back(1, 0)
    lax.fori_loop(4, 8, down_part, 0)
    forward_back(3, 0)
    forward_back(1, 1)

    def in_part(source, outgoing):
        def one(n, _):
            some = pl.ds(pl.multiple_of(n * 256, 256), 256)
            rows = fin[:, :, :, some].reshape(SLOTS, 256)
            outgoing[some, :] = dot(rows, source[...].reshape(SLOTS, FF), 0, 0).astype(BF)
            return 0

        lax.fori_loop(0, 8, one, 0)

    in_part(dhg, wg)
    forward_back(2, 0)
    forward_back(3, 1)
    forward_back(2, 1)
    in_part(dhu, wu)

    leave("gather", list(one_on.values()) + list(two.values()) + list(two_on.values()))
    to_core, to_x, own_sum = {}, {}, {}
    sums_at = (pl.ds(0, 128), pl.ds(128, 128))

    def sum_pair(k, h):
        columns = pl.ds(pl.multiple_of(h * 1024 + at(k, x) * 256, 256), 256)
        pair = dot(pmat_t[...], back[:, :, :, columns].reshape(SLOTS, 256), 1, 0)
        ours = jnp.where(c == 0, pair[:, :128], pair[:, 128:])
        theirs = jnp.where(c == 0, pair[:, 128:], pair[:, :128])
        for n in range(2):
            dz[k, :, :, n * 128 : n * 128 + 128] = ours[n * 256 : n * 256 + 256].reshape(4, CAP, 128)
        ag[k, :, sums_at[h]] = theirs.astype(BF)
        to_core[k, h] = send(ag.at[k, :, sums_at[h]], xin.at[at(k, x), :, sums_at[h]], xdev(0, 1))

    def send_sum(k, h):
        arrive("to_core", [to_core[k, h]])
        ours = [dz[k, :, :, n * 128 : n * 128 + 128].reshape(256, 128) for n in range(2)]
        part = jnp.concatenate(ours, axis=0) + xin[at(k, x), :, sums_at[h]].astype(F32)
        if k:
            ag[4 + k, :, sums_at[h]] = part.astype(BF)
            to_x[k, h] = send(ag.at[4 + k, :, sums_at[h]], xin.at[4 + x, :, sums_at[h]], xdev(k, 0))
        else:
            own_sum[h] = part

    for h in range(2):
        for k in (0,) + ORDER:
            arrive("r_two", r_two[k, h])
            arrive("t_two", t_two[k, h])
        done("own_back", own_back[h])
        sum_pair(2, h)
        sum_pair(1, h)
        send_sum(2, h)
        sum_pair(3, h)
        send_sum(1, h)
        sum_pair(0, h)
        send_sum(3, h)
        send_sum(0, h)

    slot_no = lax.broadcasted_iota(jnp.int32, (SLOTS, 128), 0) // CAP
    in_place = slot_no == lax.broadcasted_iota(jnp.int32, (SLOTS, 128), 1)
    spread = jnp.where(in_place, back[:, :, :, D:WIDE].reshape(SLOTS, 128).astype(F32), 0.0)
    values = dot(pmat_t[...], spread.astype(BF), 1, 0).T
    total_gates = jnp.zeros((TOP, TOK), F32)
    for d in range(16):
        wanted = (col + d * 8).astype(F32)
        total_gates += jnp.where(mine == wanted, values[d : d + 1, :], 0.0)
    gsend[...] = total_gates
    grecv_gates[col] = gsend[...]
    gate_sent = []
    for m in (0, 1, 3, 2):
        for f in range(2):
            if (m, f) != (0, 0):
                gate_sent.append(send(gsend, grecv_gates.at[col], xdev(m, f)))

    for h in range(2):
        total = own_sum[h]
        for k in ORDER:
            arrive("to_x", [to_x[k, h]])
            total = total + xin[4 + at(-k, x), :, sums_at[h]].astype(F32)
        out_in[:, sums_at[h]] = total.astype(BF)

    arrive("gate_sent", gate_sent)
    out_gates[...] = jnp.sum(grecv_gates[...], axis=0).astype(BF)

    leave("first", x_own + s_one + s_two)
    leave("gather", one.values())
    leave("g_sent", g_sent.values())
    for k in ORDER:
        leave("rows", p_two[k] + q_two[k])
    for h in range(2):
        for k in (0,) + ORDER:
            leave("back", r_two[k, h] + t_two[k, h])
        for k in ORDER:
            leave("back", [r_one[k, h], t_one[k, h]])
    leave("sums", gate_sent + list(to_core.values()) + list(to_x.values()))


def write_out(*refs):
    sem = refs[10]
    copies = [pltpu.make_async_copy(refs[n], refs[5 + n], sem.at[n]) for n in range(5)]
    for copy in copies:
        copy.start()
    for copy in copies:
        copy.wait()


def body(inputs, grad_output, gates, expert_ids, owner, w_gate, w_up, w_down):
    vmem, anywhere = pl.BlockSpec(memory_space=pltpu.VMEM), pl.BlockSpec(memory_space=pl.ANY)
    scratch = [
        ((8, TOK, SH), BF),
        ((16, TOK, SH), BF),
        ((16, 8, TOK), F32),
        ((8, 4, 4, CAP, SH), BF),
        ((8, 4, 4, CAP, SH), BF),
        ((4, 4, CAP, WIDE), BF),
        ((4, 4, HALF, WIDE), BF),
        ((4, 4, HALF, WIDE), BF),
        ((4, 4, CAP, WIDE), BF),
        ((4, 4, CAP, FF), F32),
        ((4, 4, CAP, FF), BF),
        ((4, 4, CAP, FF), BF),
        ((4, 4, CAP, FF), BF),
        ((256, FF), BF),
        ((256, FF), BF),
        ((4, 4, HALF, WIDE), BF),
        ((4, 4, HALF, WIDE), BF),
        ((4, 4, CAP, WIDE), BF),
        ((SLOTS, TOK), BF),
        ((TOK, SLOTS), BF),
        ((TOK, TOK), BF),
        ((32, TOK), F32),
        ((TOK, TOK), BF),
        ((8, TOK), F32),
        ((8, 8, TOK), F32),
    ]
    results = [
        ((TOK, SH), BF),
        ((TOP, TOK), BF),
        ((D, FF), BF),
        ((D, FF), BF),
        ((FF, D), BF),
    ]
    held = pl.pallas_call(
        kernel,
        out_shape=[pltpu.VMEM(shape, kind) for shape, kind in results],
        in_specs=[anywhere, anywhere, vmem, vmem, vmem, anywhere, anywhere, anywhere],
        out_specs=[vmem] * 5,
        scratch_shapes=[pltpu.VMEM(shape, kind) for shape, kind in scratch]
        + [
            pltpu.SemaphoreType.DMA((SEMS,)),
            pltpu.SemaphoreType.DMA((SEMS,)),
            pltpu.SemaphoreType.DMA((SEMS // 4,)),
        ],
        compiler_params=pltpu.CompilerParams(
            collective_id=0, has_side_effects=True, vmem_limit_bytes=53 << 20
        ),
    )(
        inputs,
        grad_output,
        expert_ids.T,
        gates.T,
        owner.reshape(1, -1),
        w_gate[0],
        w_up[0],
        w_down[0],
    )
    grad_inputs, grad_gates, grad_gate, grad_up, grad_down = pl.pallas_call(
        write_out,
        out_shape=[jax.ShapeDtypeStruct(shape, kind) for shape, kind in results],
        in_specs=[vmem] * 5,
        out_specs=[anywhere] * 5,
        scratch_shapes=[pltpu.SemaphoreType.DMA((5,))],
        compiler_params=pltpu.CompilerParams(vmem_limit_bytes=16 << 20),
    )(*[pltpu.with_memory_space_constraint(array, pltpu.VMEM) for array in held])
    return (
        grad_inputs,
        grad_gates.T,
        grad_gate[None],
        grad_up[None],
        grad_down[None],
    )


def solution(mesh):
    in_specs = (
        P("dp", "expert"),
        P("dp", "expert"),
        P("dp", None),
        P("dp", None),
        P(),
        P(("dp", "expert"), None, None),
        P(("dp", "expert"), None, None),
        P(("dp", "expert"), None, None),
    )
    out_specs = (
        P("dp", "expert"),
        P("dp", None),
        P(("dp", "expert"), None, None),
        P(("dp", "expert"), None, None),
        P(("dp", "expert"), None, None),
    )
    return jax.shard_map(body, mesh=mesh, in_specs=in_specs, out_specs=out_specs, check_vma=False)
```
